128 devices in a mesh: narrow: 4 (over z_hi, core), wide: 32 (over x, z_lo, y).
Axes of the slice: x: 4, y: 4, z: 4 (z_hi: 2, z_lo: 2; z = z_hi * 2 + z_lo), core: 2. Of those that a mesh axis runs over, the one named last changes fastest.
Arguments:
- panel: float32 [524288, 128], P(('narrow', 'wide')), may hold values from -6 to 6
- flips: int32 [524288], P(('narrow', 'wide')), may hold values from 0 to 1
- picks: int32 [8192], replicated, may hold values from 0 to 524287, as said below
Outputs:
- mixed: float32 [524288, 128], P(('narrow', 'wide'))
- sketch: float32 [8192, 128], P(('narrow', 'wide'))
- gram: float32 [128, 128], replicated
The draws below stay inside these ranges and needn't reach their ends.
Inputs may be any that keep to these rules, and one draw needn't show every extreme that they name: Split picks into aligned blocks of 64 entries, one block for each device in the order of narrow+wide. In every block, at most 1 entries name rows of any one device's block of 4096 rows, and some device's block is named exactly 1 times. Within a device's block the row is uniform; repeats may occur.
All inputs are finite; a program needn't handle non-finite values.
Results may differ from the reference program's by a relative error of at most 0.00011.
Values sent between devices are 32-bit elements; how exact they have to be, the bound alone decides.
A program may use at most 64 MiB of HBM per device.

```python
import jax
import jax.numpy as jnp
from jax import lax

COLS = 128
ROWS_DEV = 4096
SAMPLES = 8192
ROWS = 524288
N_NARROW = 4
N_WIDE = 32


def draw_picks(key, part):
    key = jax.random.fold_in(key, 7)
    devices = N_NARROW * N_WIDE
    per_block = SAMPLES // devices
    block_keys = jax.random.split(jax.random.fold_in(key, 1), devices)
    orders = jax.vmap(lambda k: jax.random.permutation(k, devices))(block_keys)
    position = jnp.arange(per_block, dtype=jnp.int32) % devices
    owners = jnp.take(orders, position, axis=1).astype(jnp.int32)
    offsets = jax.random.randint(jax.random.fold_in(key, 2), (devices, per_block), 0, ROWS_DEV, dtype=jnp.int32)
    return (owners * ROWS_DEV + offsets).reshape(SAMPLES).astype(jnp.int32)


def with_ends(entries, stream_key, low, high):
    longest = entries.shape.index(max(entries.shape))
    spots = []
    for shift in (0, 1):
        where = [jax.random.randint(jax.random.fold_in(stream_key, axis), (), 0, length) for axis, length in enumerate(entries.shape)]
        where[longest] = (where[longest] + shift) % entries.shape[longest]
        spots.append(tuple(where))
    return entries.at[spots[0]].set(low).at[spots[1]].set(high)


def level_of(key, shape, pieces, low, largest):
    loudness, own = 1.0, jax.random.fold_in(key, 6)
    for dim, parts in pieces:
        steps = jnp.exp(jax.random.uniform(jax.random.fold_in(own, dim), (parts,), jnp.float32, low / len(pieces), largest / len(pieces)))
        loudness = loudness * jnp.repeat(steps, shape[dim] // parts).reshape([-1 if axis == dim else 1 for axis in range(len(shape))])
    return loudness


def gaussian(own_key, extent, width, bound, cuts=(), kind=jnp.bfloat16):
    values = jax.random.normal(own_key, extent, jnp.float32) * width
    if len(cuts) > 0:
        values = level_of(own_key, extent, cuts, -0.22, 0.18) * values
    return jnp.clip(values, min=-bound, max=bound).astype(kind)


def setup_inputs(seed: int = 0) -> dict:
    keys = jax.random.split(jax.random.key(seed), 4)
    return {
        "panel": gaussian(keys[0], (ROWS, COLS), 1.0, 6.0, ((0, 128),), jnp.float32),
        "flips": with_ends(jax.random.randint(keys[1], (ROWS,), 0, 2), jax.random.fold_in(keys[1], 1), 0, 1).astype(jnp.int32),
        "picks": draw_picks(jax.random.fold_in(keys[3], 71), 0),
    }


def hadamard(order):
    index = jnp.arange(order, dtype=jnp.int32)
    both = index[:, None] & index[None, :]
    parity = jnp.zeros((order, order), jnp.int32)
    level = 0
    while (1 << level) < order:
        parity = parity ^ ((both >> level) & 1)
        level += 1
    return (1 - 2 * parity).astype(jnp.float32)


def reference(panel, flips, picks):
    devices = N_NARROW * N_WIDE
    inner = ROWS_DEV // 64
    signed = panel * (1 - 2 * flips).astype(jnp.float32)[:, None]
    shaped = signed.reshape(devices, 64, inner, COLS)
    shaped = jnp.einsum("ap,dpqc->daqc", hadamard(64), shaped, precision=lax.Precision.HIGHEST)
    shaped = jnp.einsum("bq,daqc->dabc", hadamard(inner), shaped, precision=lax.Precision.HIGHEST)
    shaped = jnp.einsum("ed,dabc->eabc", hadamard(devices), shaped, precision=lax.Precision.HIGHEST)
    mixed = shaped.reshape(ROWS, COLS) * (1.0 / (float(ROWS) ** 0.5))
    sketch = jnp.take(mixed, picks, axis=0)
    gram = jnp.dot(sketch.T, sketch, precision=lax.Precision.HIGHEST, preferred_element_type=jnp.float32) / SAMPLES
    return mixed, sketch, gram
```

```python
import functools

import jax
import jax.numpy as jnp
from jax import lax
from jax.experimental import pallas as pl
from jax.experimental.pallas import tpu as pltpu
from jax.sharding import PartitionSpec as P

MESH = pl.DeviceIdType.MESH
DEV = 128
ROWS = 4096
COLS = 128
CHUNK = 32
HALF = 16
SCALE = 1.0 / float(ROWS * DEV) ** 0.5


def place(flat):
    return (flat // 32, flat % 32)


def partner(me, k):
    off = (k * 37) & 127
    y = (me + off) & 3
    z = (((me >> 2) & 1) + ((me >> 5) & 2) + (off >> 2)) & 3
    x = ((me >> 3) + (off >> 4)) & 3
    core = ((me >> 5) ^ (off >> 6)) & 1
    return y + (z & 1) * 4 + x * 8 + core * 32 + (z >> 1) * 64


def each_partner(me, body):
    def step(k, carry):
        body(partner(me, k))
        return carry

    lax.fori_loop(1, DEV, step, 0)


def butterfly(values):
    values = list(values)
    apart = 1
    while apart < len(values):
        for i in range(len(values)):
            if i & apart == 0:
                a, b = values[i], values[i + apart]
                values[i], values[i + apart] = a + b, a - b
        apart *= 2
    return values


def local_transform(x_ref, signs_ref, t_ref):
    def first(g, carry):
        base = pl.multiple_of(g * 128, 128)
        pick = (lax.broadcasted_iota(jnp.int32, (32, COLS), 0) == g).astype(jnp.float32)
        sign = jnp.dot(signs_ref[...], pick, preferred_element_type=jnp.float32)
        rows = x_ref[pl.ds(base, 128), :] * sign
        out = butterfly([rows[8 * m : 8 * m + 8] for m in range(16)])
        for m in range(16):
            t_ref[pl.ds(base + 8 * m, 8), :] = out[m]
        return carry

    lax.fori_loop(0, 32, first, 0)

    def second(g, carry):
        base = (g // 2) * 256 + (g % 2) * 64
        spots = [base + 128 * h + k for h in range(2) for k in range(8)]
        out = butterfly([t_ref[pl.ds(s, 8, stride=8), :] for s in spots])
        for s, value in zip(spots, out):
            t_ref[pl.ds(s, 8, stride=8), :] = value
        return carry

    lax.fori_loop(0, 32, second, 0)

    def third(g, carry):
        spots = [pl.multiple_of(g * 8 + 256 * m, 8) for m in range(16)]
        out = butterfly([t_ref[pl.ds(s, 8), :] for s in spots])
        for s, value in zip(spots, out):
            t_ref[pl.ds(s, 8), :] = value
        return carry

    lax.fori_loop(0, 32, third, 0)


def device_transform(half, src_ref, dst_ref):
    def low(g, carry):
        for u in range(2):
            rows = pl.ds(half * HALF + 8 * u, 8)
            out = butterfly([src_ref[g * 16 + m, rows, :] for m in range(16)])
            for m in range(16):
                dst_ref[g * 16 + m, rows, :] = out[m]
        return carry

    lax.fori_loop(0, 8, low, 0)

    def high(g, carry):
        for u in range(2):
            rows = pl.ds(half * HALF + 8 * u, 8)
            out = butterfly([dst_ref[g + 16 * m, rows, :] for m in range(8)])
            for m in range(8):
                dst_ref[g + 16 * m, rows, :] = out[m] * SCALE
        return carry

    lax.fori_loop(0, 16, high, 0)


def counts_of(me, picks_ref):
    def step(k, total):
        p = picks_ref[pl.ds(k, 1), :]
        here = ((p >> 5) & 127) == me
        q = (p >> 12) * CHUNK + (p & 31)
        hi = jnp.where(here, q >> 7, -1)
        lo = q & 127
        a = (lax.broadcasted_iota(jnp.int32, (32, 128), 0) == hi).astype(jnp.float32)
        b = (lax.broadcasted_iota(jnp.int32, (128, 128), 0) == lo).astype(jnp.float32)
        return total + lax.dot_general(
            a, b, (((1,), (1,)), ((), ())), preferred_element_type=jnp.float32
        )

    return lax.fori_loop(0, 64, step, jnp.zeros((32, 128), jnp.float32))


def kernel(
    panel_ref, flips_ref, picks_ref, picks_any,
    mixed_ref, sketch_ref, gram_ref,
    x_ref, t_ref, in_ref, done_ref, signs_ref, counts_ref, wanted_ref, wanted_sm, mine_sm,
    sk_out, sk_in, gp_out, gp_in, gs_out, gs_in,
    load_sem, small_sem, own_sem, p1s, p1r, p2s, p2r, sks, skr, gps, gpr, gss, gsr,
):
    me = lax.axis_index("narrow") * 32 + lax.axis_index("wide")
    load = pltpu.make_async_copy(panel_ref, x_ref, load_sem)
    load.start()
    mine = pltpu.make_async_copy(picks_any.at[me // 2], mine_sm, small_sem.at[0])
    mine.start()

    barrier = pltpu.get_barrier_semaphore()
    each_partner(
        me,
        lambda d: pl.semaphore_signal(barrier, inc=1, device_id=place(d), device_id_type=MESH),
    )

    p = picks_ref[...]
    lane = lax.broadcasted_iota(jnp.int32, p.shape, 1)
    local = jnp.where((p >> 12) == me, p & (ROWS - 1), 0)
    even = jnp.max(jnp.where(lane < 64, local, 0), axis=1, keepdims=True)
    odd = jnp.max(jnp.where(lane < 64, 0, local), axis=1, keepdims=True)
    wanted_ref[...] = jnp.where(lane == 0, even, odd)
    wanted = pltpu.make_async_copy(wanted_ref, wanted_sm, small_sem.at[1])
    wanted.start()

    signs_ref[...] = (1 - 2 * flips_ref[...]).astype(jnp.float32).T
    load.wait()
    local_transform(x_ref, signs_ref, t_ref)
    pl.semaphore_wait(barrier, DEV - 1)

    def rows_of(d, half):
        return pl.ds(pl.multiple_of(d * CHUNK + half * HALF, HALF), HALF)

    def send_in(half):
        def one(d):
            pltpu.make_async_remote_copy(
                t_ref.at[rows_of(d, half)], in_ref.at[me, pl.ds(half * HALF, HALF)],
                p1s.at[half], p1r.at[half], device_id=place(d), device_id_type=MESH,
            ).start()

        each_partner(me, one)

    def send_back(half):
        def one(d):
            pltpu.make_async_remote_copy(
                done_ref.at[d, pl.ds(half * HALF, HALF)], mixed_ref.at[rows_of(me, half)],
                p2s.at[half], p2r.at[half], device_id=place(d), device_id_type=MESH,
            ).start()

        each_partner(me, one)

    others = pl.ds(0, (DEV - 1) * HALF)

    def wait_bytes(sem):
        pltpu.make_async_copy(x_ref.at[others], t_ref.at[others], sem).wait()

    send_in(0)
    send_in(1)
    in_ref[me] = t_ref[pl.ds(pl.multiple_of(me * CHUNK, CHUNK), CHUNK), :]
    counts_ref[...] = counts_of(me, picks_ref)

    wait_bytes(p1r.at[0])
    device_transform(0, in_ref, done_ref)
    send_back(0)
    wait_bytes(p1r.at[1])
    device_transform(1, in_ref, done_ref)
    mixed_ref[pl.ds(pl.multiple_of(me * CHUNK, CHUNK), CHUNK), :] = done_ref[me]

    def gram_step(g, total):
        rows = done_ref[pl.ds(g * 4, 4)].reshape(128, COLS)
        left = rows.T * counts_ref[pl.ds(g, 1), :]
        return total + jnp.dot(
            left, rows, precision=lax.Precision.HIGHEST, preferred_element_type=jnp.float32
        )

    part = lax.fori_loop(0, 32, gram_step, jnp.zeros((COLS, COLS), jnp.float32))
    gp_out[...] = part.reshape(COLS, 1, COLS)

    def row_to(src, dst, send, recv, d):
        pltpu.make_async_remote_copy(
            src, dst, send, recv, device_id=place(d), device_id_type=MESH
        ).start()

    def wait_rows(sem):
        pltpu.make_async_copy(
            sk_out.at[pl.ds(0, DEV - 1)], sk_in.at[pl.ds(0, DEV - 1)], sem
        ).wait()

    each_partner(me, lambda d: row_to(gp_out.at[d], gp_in.at[me], gps, gpr, d))
    gp_in[me] = gp_out[me]
    send_back(1)

    wait_rows(gpr)
    gs_out[...] = jnp.sum(gp_in[...], axis=0, keepdims=True) * (1.0 / 8192.0)
    each_partner(me, lambda d: row_to(gs_out.at[0], gs_in.at[me], gss, gsr, d))
    gs_in[me] = gs_out[0]

    wait_bytes(p2r.at[0])
    wait_bytes(p2r.at[1])
    wanted.wait()

    def row_for(d):
        sk_out[d] = mixed_ref[pl.ds(wanted_sm[d // 2, d % 2], 1), :]

    def send_row(d):
        row_for(d)
        row_to(sk_out.at[d], sk_in.at[me], sks, skr, d)

    each_partner(me, send_row)
    row_for(me)
    sk_in[me] = sk_out[me]

    wait_rows(gsr)
    gram_ref[...] = gs_in[...].reshape(COLS, COLS)
    mine.wait()
    wait_rows(skr)
    start = (me % 2) * 64

    def pick_row(i, carry):
        owner = (mine_sm[start + i] >> 12) & (DEV - 1)
        sketch_ref[pl.ds(i, 1), :] = sk_in[owner]
        return carry

    lax.fori_loop(0, 64, pick_row, 0)
    for half in range(2):
        wait_bytes(p1s.at[half])
        wait_bytes(p2s.at[half])
    wait_rows(gps)
    wait_rows(gss)
    wait_rows(sks)


def on_device(panel, flips, picks):
    vmem = pl.BlockSpec(memory_space=pltpu.VMEM)
    hbm = pl.BlockSpec(memory_space=pl.ANY)
    dma = pltpu.SemaphoreType.DMA
    f32 = jnp.float32
    row = pltpu.VMEM((DEV, 1, COLS), f32)
    picks = picks.reshape(64, 128)
    return pl.pallas_call(
        kernel,
        out_shape=(
            jax.ShapeDtypeStruct((ROWS, COLS), f32),
            jax.ShapeDtypeStruct((64, COLS), f32),
            jax.ShapeDtypeStruct((COLS, COLS), f32),
        ),
        in_specs=[hbm, vmem, vmem, hbm],
        out_specs=(vmem, vmem, vmem),
        scratch_shapes=[
            pltpu.VMEM((ROWS, COLS), f32),
            pltpu.VMEM((ROWS, COLS), f32),
            pltpu.VMEM((DEV, CHUNK, COLS), f32),
            pltpu.VMEM((DEV, CHUNK, COLS), f32),
            pltpu.VMEM((128, 32), f32),
            pltpu.VMEM((32, 128), f32),
            pltpu.VMEM((64, 128), jnp.int32),
            pltpu.SMEM((64, 128), jnp.int32),
            pltpu.SMEM((128,), jnp.int32),
            row, row, row, row, pltpu.VMEM((1, 1, COLS), f32), row,
            dma, dma((2,)), dma, dma((2,)), dma((2,)), dma((2,)), dma((2,)),
            dma, dma, dma, dma, dma, dma,
        ],
        name="sketch",
        compiler_params=pltpu.CompilerParams(
            collective_id=1, has_side_effects=True, vmem_limit_bytes=40 * 2**20
        ),
    )(panel, flips.reshape(32, 128), picks, picks)


def solution(mesh):
    both = ("narrow", "wide")
    return jax.shard_map(
        on_device,
        mesh=mesh,
        in_specs=(P(both, None), P(both), P()),
        out_specs=(P(both, None), P(both, None), P()),
        check_vma=False,
    )
```

```python
import functools

import jax
import jax.numpy as jnp
from jax import lax
from jax.experimental import pallas as pl
from jax.experimental.pallas import tpu as pltpu
from jax.sharding import PartitionSpec as P

MESH = pl.DeviceIdType.MESH
DEV = 128
ROWS = 4096
COLS = 128
CHUNK = 32
HALF = 16
LOADS = 4
SCALE = 1.0 / float(ROWS * DEV) ** 0.5


def place(flat):
    return (flat // 32, flat % 32)


def partner(me, k):
    off = (k * 37) & 127
    y = (me + off) & 3
    z = (((me >> 2) & 1) + ((me >> 5) & 2) + (off >> 2)) & 3
    x = ((me >> 3) + (off >> 4)) & 3
    core = ((me >> 5) ^ (off >> 6)) & 1
    return y + (z & 1) * 4 + x * 8 + core * 32 + (z >> 1) * 64


def each_partner(me, body):
    def step(k, carry):
        body(partner(me, k))
        return carry

    lax.fori_loop(1, DEV, step, 0)


def butterfly(values):
    values = list(values)
    apart = 1
    while apart < len(values):
        for i in range(len(values)):
            if i & apart == 0:
                a, b = values[i], values[i + apart]
                values[i], values[i + apart] = a + b, a - b
        apart *= 2
    return values


def first_pass(x_ref, signs, t_ref, g):
    rows = x_ref[g * 128 : g * 128 + 128, :] * signs[:, g : g + 1]
    out = butterfly([rows[8 * m : 8 * m + 8] for m in range(16)])
    for m in range(16):
        t_ref[g * 128 + 8 * m : g * 128 + 8 * m + 8, :] = out[m]


def second_pass(t_ref):
    def step(g, carry):
        base = (g // 2) * 256 + (g % 2) * 64
        spots = [base + 128 * h + k for h in range(2) for k in range(8)]
        out = butterfly([t_ref[pl.ds(s, 8, stride=8), :] for s in spots])
        for s, value in zip(spots, out):
            t_ref[pl.ds(s, 8, stride=8), :] = value
        return carry

    lax.fori_loop(0, 32, step, 0, unroll=4)


def third_pass(half, t_ref):
    def step(g, carry):
        base = pl.multiple_of((g % 2) * 8 + half * HALF + (g // 2) * CHUNK, 8)
        spots = [base + 256 * m for m in range(16)]
        out = butterfly([t_ref[pl.ds(s, 8), :] for s in spots])
        for s, value in zip(spots, out):
            t_ref[pl.ds(s, 8), :] = value
        return carry

    lax.fori_loop(0, 16, step, 0, unroll=4)


def device_transform(half, src_ref, dst_ref):
    def low(g, carry):
        for u in range(2):
            rows = pl.ds(half * HALF + 8 * u, 8)
            out = butterfly([src_ref[g * 16 + m, rows, :] for m in range(16)])
            for m in range(16):
                dst_ref[g * 16 + m, rows, :] = out[m]
        return carry

    lax.fori_loop(0, 8, low, 0, unroll=2)

    def high(g, carry):
        for u in range(2):
            rows = pl.ds(half * HALF + 8 * u, 8)
            out = butterfly([dst_ref[g + 16 * m, rows, :] for m in range(8)])
            for m in range(8):
                dst_ref[g + 16 * m, rows, :] = out[m] * SCALE
        return carry

    lax.fori_loop(0, 16, high, 0, unroll=4)


def counts_of(me, picks_ref):
    def step(k, total):
        p = picks_ref[pl.ds(k, 1), :]
        here = ((p >> 5) & 127) == me
        q = ((p >> 4) & 1) * (DEV * HALF) + (p >> 12) * HALF + (p & 15)
        hi = jnp.where(here, q >> 7, -1)
        lo = q & 127
        a = (lax.broadcasted_iota(jnp.int32, (32, 128), 0) == hi).astype(jnp.float32)
        b = (lax.broadcasted_iota(jnp.int32, (128, 128), 0) == lo).astype(jnp.float32)
        return total + lax.dot_general(
            a, b, (((1,), (1,)), ((), ())), preferred_element_type=jnp.float32
        )

    return lax.fori_loop(0, 64, step, jnp.zeros((32, 128), jnp.float32))


def kernel(
    panel_ref, flips_hbm, picks_hbm,
    mixed_ref, sketch_ref, gram_ref,
    x_ref, t_ref, in_ref, done_ref, flips_ref, picks_ref, counts_ref, part_ref, wanted_ref, wanted_sm, mine_sm,
    row_out, row_in, gp_out, gp_in,
    load_sem, small_sem, p1s, p1r, p2s, p2r, rows_s, rows_r, gps, gpr,
):
    me = lax.axis_index("narrow") * 32 + lax.axis_index("wide")
    small = [
        pltpu.make_async_copy(flips_hbm, flips_ref, small_sem.at[0]),
        pltpu.make_async_copy(picks_hbm, picks_ref, small_sem.at[1]),
        pltpu.make_async_copy(picks_hbm.at[me // 2], mine_sm, small_sem.at[2]),
    ]
    for copy in small:
        copy.start()
    loads = []
    for i in range(LOADS):
        rows = pl.ds(i * (ROWS // LOADS), ROWS // LOADS)
        loads.append(pltpu.make_async_copy(panel_ref.at[rows], x_ref.at[rows], load_sem.at[i]))
        loads[-1].start()

    barrier = pltpu.get_barrier_semaphore()
    small[0].wait()
    signs = (1 - 2 * flips_ref[...]).astype(jnp.float32).T
    for g in range(32):
        for k in range(4 * g, 4 * g + 4):
            if k > 0:
                pl.semaphore_signal(
                    barrier, inc=1, device_id=place(partner(me, k)), device_id_type=MESH
                )
        if g % (32 // LOADS) == 0:
            loads[g // (32 // LOADS)].wait()
        first_pass(x_ref, signs, t_ref, g)
    second_pass(t_ref)
    third_pass(0, t_ref)
    pl.semaphore_wait(barrier, DEV - 1)

    def rows_of(d, half):
        return pl.ds(pl.multiple_of(d * CHUNK + half * HALF, HALF), HALF)

    def send_in(half):
        def one(d):
            pltpu.make_async_remote_copy(
                t_ref.at[rows_of(d, half)], in_ref.at[me, pl.ds(half * HALF, HALF)],
                p1s.at[half], p1r.at[half], device_id=place(d), device_id_type=MESH,
            ).start()

        each_partner(me, one)

    def send_back(half):
        def one(d):
            pltpu.make_async_remote_copy(
                done_ref.at[d, pl.ds(half * HALF, HALF)], mixed_ref.at[rows_of(me, half)],
                p2s.at[half], p2r.at[half], device_id=place(d), device_id_type=MESH,
            ).start()

        each_partner(me, one)

    others = pl.ds(0, (DEV - 1) * HALF)

    def wait_bytes(sem):
        pltpu.make_async_copy(x_ref.at[others], t_ref.at[others], sem).wait()

    def add_gram(half):
        def step(g, total):
            rows = done_ref[pl.ds(g * 8, 8), pl.ds(half * HALF, HALF), :].reshape(128, COLS)
            left = rows.T * counts_ref[pl.ds(half * 16 + g, 1), :]
            return total + jnp.dot(
                left, rows, precision=lax.Precision.HIGHEST, preferred_element_type=jnp.float32
            )

        part_ref[...] = lax.fori_loop(0, 16, step, part_ref[...])

    send_in(0)
    third_pass(1, t_ref)
    send_in(1)
    in_ref[me] = t_ref[pl.ds(pl.multiple_of(me * CHUNK, CHUNK), CHUNK), :]

    small[1].wait()
    p = picks_ref[...]
    lane = lax.broadcasted_iota(jnp.int32, p.shape, 1)
    local = jnp.where((p >> 12) == me, p & (ROWS - 1), 0)
    even = jnp.max(jnp.where(lane < 64, local, 0), axis=1, keepdims=True)
    odd = jnp.max(jnp.where(lane < 64, 0, local), axis=1, keepdims=True)
    wanted_ref[...] = jnp.where(lane == 0, even, odd)
    wanted = pltpu.make_async_copy(wanted_ref, wanted_sm, small_sem.at[1])
    wanted.start()
    counts_ref[...] = counts_of(me, picks_ref)
    part_ref[...] = jnp.zeros_like(part_ref)

    wait_bytes(p1r.at[0])
    device_transform(0, in_ref, done_ref)
    send_back(0)
    add_gram(0)
    wait_bytes(p1r.at[1])
    device_transform(1, in_ref, done_ref)
    send_back(1)
    mixed_ref[pl.ds(pl.multiple_of(me * CHUNK, CHUNK), CHUNK), :] = done_ref[me]
    add_gram(1)
    gp_out[...] = part_ref[...].reshape(COLS, 1, COLS)

    def send(src, dst, send_sem, recv_sem, d):
        pltpu.make_async_remote_copy(
            src, dst, send_sem, recv_sem, device_id=place(d), device_id_type=MESH
        ).start()

    def wait_rows(ref, sem):
        pltpu.make_async_copy(ref.at[pl.ds(0, DEV - 1)], ref.at[pl.ds(0, DEV - 1)], sem).wait()

    each_partner(me, lambda d: send(gp_out.at[d], gp_in.at[me], gps, gpr, d))
    gp_in[me] = gp_out[me]
    wait_rows(gp_in, gpr)
    gram_row = jnp.sum(gp_in[...], axis=0, keepdims=True) * (1.0 / 8192.0)
    row_out[:, 1:2, :] = jnp.broadcast_to(gram_row, (DEV, 1, COLS))

    wait_bytes(p2r.at[0])
    wait_bytes(p2r.at[1])
    wanted.wait()

    def row_for(d):
        row_out[d, 0:1, :] = mixed_ref[pl.ds(wanted_sm[d // 2, d % 2], 1), :]

    def send_row(d):
        row_for(d)
        send(row_out.at[d], row_in.at[me], rows_s, rows_r, d)

    each_partner(me, send_row)
    row_for(me)
    row_in[me] = row_out[me]

    small[2].wait()
    wait_rows(row_in, rows_r)
    gram_ref[...] = row_in[:, 1, :]
    start = (me % 2) * 64

    def pick_row(i, carry):
        owner = (mine_sm[start + i] >> 12) & (DEV - 1)
        sketch_ref[pl.ds(i, 1), :] = row_in[owner, 0:1, :]
        return carry

    lax.fori_loop(0, 64, pick_row, 0, unroll=8)
    for half in range(2):
        wait_bytes(p1s.at[half])
        wait_bytes(p2s.at[half])
    wait_rows(gp_in, gps)
    wait_rows(row_in, rows_s)


def leave_kernel(mixed_ref, sketch_ref, gram_ref, mixed_out, sketch_out, gram_out, sems):
    pairs = ((mixed_ref, mixed_out), (sketch_ref, sketch_out), (gram_ref, gram_out))
    copies = [pltpu.make_async_copy(a, b, sems.at[i]) for i, (a, b) in enumerate(pairs)]
    for copy in copies:
        copy.start()
    for copy in copies:
        copy.wait()


def on_device(panel, flips, picks):
    vmem = pl.BlockSpec(memory_space=pltpu.VMEM)
    hbm = pl.BlockSpec(memory_space=pltpu.HBM)
    dma = pltpu.SemaphoreType.DMA
    f32, i32 = jnp.float32, jnp.int32
    shapes = ((ROWS, COLS), (64, COLS), (COLS, COLS))
    parts = pl.pallas_call(
        kernel,
        out_shape=tuple(pltpu.VMEM(shape, f32) for shape in shapes),
        in_specs=[hbm, hbm, hbm],
        out_specs=(vmem, vmem, vmem),
        scratch_shapes=[
            pltpu.VMEM((ROWS, COLS), f32),
            pltpu.VMEM((ROWS, COLS), f32),
            pltpu.VMEM((DEV, CHUNK, COLS), f32),
            pltpu.VMEM((DEV, CHUNK, COLS), f32),
            pltpu.VMEM((32, 128), i32),
            pltpu.VMEM((64, 128), i32),
            pltpu.VMEM((32, 128), f32),
            pltpu.VMEM((COLS, COLS), f32),
            pltpu.VMEM((64, 128), i32),
            pltpu.SMEM((64, 128), i32),
            pltpu.SMEM((128,), i32),
            pltpu.VMEM((DEV, 2, COLS), f32),
            pltpu.VMEM((DEV, 2, COLS), f32),
            pltpu.VMEM((DEV, 1, COLS), f32),
            pltpu.VMEM((DEV, 1, COLS), f32),
            dma((LOADS,)), dma((3,)), dma((2,)), dma((2,)), dma((2,)), dma((2,)),
            dma, dma, dma, dma,
        ],
        name="sketch",
        compiler_params=pltpu.CompilerParams(
            collective_id=1, has_side_effects=True, vmem_limit_bytes=56 * 2**20
        ),
    )(panel, flips.reshape(32, 128), picks.reshape(64, 128))
    return pl.pallas_call(
        leave_kernel,
        out_shape=tuple(jax.ShapeDtypeStruct(shape, f32) for shape in shapes),
        in_specs=[vmem, vmem, vmem],
        out_specs=(hbm, hbm, hbm),
        scratch_shapes=[dma((3,))],
        name="leave",
    )(*parts)


def solution(mesh):
    both = ("narrow", "wide")
    return jax.shard_map(
        on_device,
        mesh=mesh,
        in_specs=(P(both, None), P(both), P()),
        out_specs=(P(both, None), P(both, None), P()),
        check_vma=False,
    )
```

```python
import itertools

import jax
import jax.numpy as jnp
from jax import lax
from jax.experimental import pallas as pl
from jax.experimental.pallas import tpu as pltpu
from jax.sharding import PartitionSpec as P

MESH = pl.DeviceIdType.MESH
DEV = 128
ROWS = 4096
COLS = 128
CHUNK = 32
HALF = 16
LOADS = 4
SCALE = 1.0 / float(ROWS * DEV) ** 0.5


def offsets():
    rest = [o for o in itertools.product(range(4), range(4), range(4), range(2)) if any(o)]
    used = [0] * 6
    order = []

    def load(o):
        out = [0] * 6
        for i in range(3):
            out[2 * i] = (0, 1, 1, 0)[o[i]]
            out[2 * i + 1] = (0, 0, 1, 1)[o[i]]
        return out

    def cost(o):
        total = [u + w for u, w in zip(used, load(o))]
        return -sum(load(o)), max(total) - min(total), max(total)

    while rest:
        best = min(rest, key=cost)
        rest.remove(best)
        order.append(best)
        used = [u + w for u, w in zip(used, load(best))]
    return order


OFFSETS = offsets()


class Place:
    def __init__(self):
        self.narrow, self.wide = lax.axis_index("narrow"), lax.axis_index("wide")
        self.me = self.narrow * 32 + self.wide
        y, z_lo, x = self.wide & 3, (self.wide >> 2) & 1, self.wide >> 3
        core, z = self.narrow & 1, (self.narrow >> 1) * 2 + z_lo
        self.xs = [((x + i) & 3) * 8 for i in range(4)]
        self.ys = [(y + i) & 3 for i in range(4)]
        self.zs = [((z + i) & 1) * 4 for i in range(4)]
        self.zn = [(((z + i) >> 1) & 1) * 2 for i in range(4)]
        self.cs = [core, 1 - core]

    def others(self):
        for dx, dy, dz, dc in OFFSETS:
            narrow, wide = self.zn[dz] + self.cs[dc], self.xs[dx] + self.ys[dy] + self.zs[dz]
            yield narrow * 32 + wide, (narrow, wide)


def butterfly(values):
    values = list(values)
    apart = 1
    while apart < len(values):
        for i in range(len(values)):
            if i & apart == 0:
                a, b = values[i], values[i + apart]
                values[i], values[i + apart] = a + b, a - b
        apart *= 2
    return values


def first_pass(x_ref, signs, t_ref, g):
    rows = x_ref[g * 128 : g * 128 + 128, :] * signs[:, g : g + 1]
    out = butterfly([rows[8 * m : 8 * m + 8] for m in range(16)])
    for m in range(16):
        t_ref[g * 128 + 8 * m : g * 128 + 8 * m + 8, :] = out[m]


def second_pass(t_ref):
    def step(g, carry):
        base = (g // 2) * 256 + (g % 2) * 64
        spots = [base + 128 * h + k for h in range(2) for k in range(8)]
        out = butterfly([t_ref[pl.ds(s, 8, stride=8), :] for s in spots])
        for s, value in zip(spots, out):
            t_ref[pl.ds(s, 8, stride=8), :] = value
        return carry

    lax.fori_loop(0, 32, step, 0, unroll=4)


def third_pass(half, t_ref):
    def step(g, carry):
        base = pl.multiple_of((g % 2) * 8 + half * HALF + (g // 2) * CHUNK, 8)
        spots = [base + 256 * m for m in range(16)]
        out = butterfly([t_ref[pl.ds(s, 8), :] for s in spots])
        for s, value in zip(spots, out):
            t_ref[pl.ds(s, 8), :] = value
        return carry

    lax.fori_loop(0, 16, step, 0, unroll=4)


def device_transform(half, src_ref, dst_ref):
    def low(g, carry):
        for u in range(2):
            rows = pl.ds(half * HALF + 8 * u, 8)
            out = butterfly([src_ref[g * 16 + m, rows, :] for m in range(16)])
            for m in range(16):
                dst_ref[g * 16 + m, rows, :] = out[m]
        return carry

    lax.fori_loop(0, 8, low, 0, unroll=2)

    def high(g, carry):
        for u in range(2):
            rows = pl.ds(half * HALF + 8 * u, 8)
            out = butterfly([dst_ref[g + 16 * m, rows, :] for m in range(8)])
            for m in range(8):
                dst_ref[g + 16 * m, rows, :] = out[m] * SCALE
        return carry

    lax.fori_loop(0, 16, high, 0, unroll=4)


def counts_of(me, picks_ref):
    def step(k, total):
        p = picks_ref[pl.ds(k, 1), :]
        here = ((p >> 5) & 127) == me
        q = ((p >> 4) & 1) * (DEV * HALF) + (p >> 12) * HALF + (p & 15)
        hi = jnp.where(here, q >> 7, -1)
        lo = q & 127
        a = (lax.broadcasted_iota(jnp.int32, (32, 128), 0) == hi).astype(jnp.float32)
        b = (lax.broadcasted_iota(jnp.int32, (128, 128), 0) == lo).astype(jnp.float32)
        return total + lax.dot_general(
            a, b, (((1,), (1,)), ((), ())), preferred_element_type=jnp.float32
        )

    return lax.fori_loop(0, 64, step, jnp.zeros((32, 128), jnp.float32))


def kernel(
    panel_ref, flips_hbm, picks_hbm,
    mixed_ref, sketch_ref, gram_ref,
    x_ref, t_ref, in_ref, done_ref, flips_ref, picks_ref, counts_ref, part_ref, wanted_ref, wanted_sm, mine_sm,
    row_out, row_in, gp_out, gp_in,
    load_sem, small_sem, p1s, p1r, p2s, p2r, gps, gpr, rows_s, rows_r,
):
    here = Place()
    me = here.me
    small = [
        pltpu.make_async_copy(flips_hbm, flips_ref, small_sem.at[0]),
        pltpu.make_async_copy(picks_hbm, picks_ref, small_sem.at[1]),
        pltpu.make_async_copy(picks_hbm.at[me >> 1], mine_sm, small_sem.at[2]),
    ]
    small[0].start()
    loads = []
    for i in range(LOADS):
        rows = pl.ds(i * (ROWS // LOADS), ROWS // LOADS)
        loads.append(pltpu.make_async_copy(panel_ref.at[rows], x_ref.at[rows], load_sem.at[i]))
        loads[-1].start()
    small[1].start()
    small[2].start()
    barrier = pltpu.get_barrier_semaphore()
    for _, spot in here.others():
        pl.semaphore_signal(barrier, inc=1, device_id=spot, device_id_type=MESH)

    small[0].wait()
    signs = (1 - 2 * flips_ref[...]).astype(jnp.float32).T
    for g in range(32):
        if g % (32 // LOADS) == 0:
            loads[g // (32 // LOADS)].wait()
        first_pass(x_ref, signs, t_ref, g)
    second_pass(t_ref)
    third_pass(0, t_ref)
    pl.semaphore_wait(barrier, DEV - 1)

    def rows_of(d, half):
        return pl.ds(pl.multiple_of(d * CHUNK + half * HALF, HALF), HALF)

    def send(src, dst, send_sem, recv_sem, spot):
        pltpu.make_async_remote_copy(
            src, dst, send_sem, recv_sem, device_id=spot, device_id_type=MESH
        ).start()

    def send_in(half):
        part = pl.ds(half * HALF, HALF)
        for d, spot in here.others():
            send(t_ref.at[rows_of(d, half)], in_ref.at[me, part], p1s.at[half], p1r.at[half], spot)

    def send_back(half):
        part = pl.ds(half * HALF, HALF)
        for d, spot in here.others():
            send(done_ref.at[d, part], mixed_ref.at[rows_of(me, half)], p2s.at[half], p2r.at[half], spot)

    def wait_bytes(sem):
        others = pl.ds(0, (DEV - 1) * HALF)
        pltpu.make_async_copy(x_ref.at[others], t_ref.at[others], sem).wait()

    def wait_rows(ref, sem):
        pltpu.make_async_copy(ref.at[pl.ds(0, DEV - 1)], ref.at[pl.ds(0, DEV - 1)], sem).wait()

    def add_gram(half):
        def step(g, total):
            rows = done_ref[pl.ds(g * 8, 8), pl.ds(half * HALF, HALF), :].reshape(128, COLS)
            left = rows.T * counts_ref[pl.ds(half * 16 + g, 1), :]
            return total + jnp.dot(
                left, rows, precision=lax.Precision.HIGHEST, preferred_element_type=jnp.float32
            )

        part_ref[...] = lax.fori_loop(0, 16, step, part_ref[...])

    send_in(0)
    third_pass(1, t_ref)
    send_in(1)
    in_ref[me] = t_ref[pl.ds(pl.multiple_of(me * CHUNK, CHUNK), CHUNK), :]

    small[1].wait()
    p = picks_ref[...]
    lane = lax.broadcasted_iota(jnp.int32, p.shape, 1)
    local = jnp.where((p >> 12) == me, p & (ROWS - 1), 0)
    even = jnp.max(jnp.where(lane < 64, local, 0), axis=1, keepdims=True)
    odd = jnp.max(jnp.where(lane < 64, 0, local), axis=1, keepdims=True)
    wanted_ref[...] = jnp.where(lane == 0, even, odd)
    wanted = pltpu.make_async_copy(wanted_ref, wanted_sm, small_sem.at[1])
    wanted.start()
    counts_ref[...] = counts_of(me, picks_ref)
    part_ref[...] = jnp.zeros_like(part_ref)

    wait_bytes(p1r.at[0])
    device_transform(0, in_ref, done_ref)
    send_back(0)
    add_gram(0)
    wait_bytes(p1r.at[1])
    device_transform(1, in_ref, done_ref)
    add_gram(1)
    gp_out[...] = part_ref[...].reshape(DEV, 1, COLS)
    for d, spot in here.others():
        send(gp_out.at[d], gp_in.at[me], gps, gpr, spot)
    send_back(1)
    gp_in[me] = gp_out[me]
    mixed_ref[pl.ds(pl.multiple_of(me * CHUNK, CHUNK), CHUNK), :] = done_ref[me]
    wait_rows(gp_in, gpr)
    gram_row = jnp.sum(gp_in[...], axis=0, keepdims=True) * (1.0 / 8192.0)
    row_out[:, 1] = jnp.broadcast_to(gram_row, (DEV, 1, COLS))

    wanted.wait()
    wait_bytes(p2r.at[0])
    wait_bytes(p2r.at[1])

    def gather(k, carry):
        for j in range(2):
            row_out[2 * k + j, 0] = mixed_ref[pl.ds(wanted_sm[k, j], 1), :]
        return carry

    lax.fori_loop(0, DEV // 2, gather, 0, unroll=8)
    for d, spot in here.others():
        send(row_out.at[d], row_in.at[me], rows_s, rows_r, spot)
    row_in[me] = row_out[me]
    small[2].wait()
    for half in range(2):
        wait_bytes(p1s.at[half])
        wait_bytes(p2s.at[half])
    wait_rows(gp_in, gps)
    wait_rows(row_in, rows_r)
    start = (me & 1) * 64

    def pick_row(i, carry):
        sketch_ref[pl.ds(i, 1), :] = row_in[(mine_sm[start + i] >> 12) & (DEV - 1), 0]
        return carry

    lax.fori_loop(0, 64, pick_row, 0, unroll=16)
    gram_ref[...] = row_in[:, 1].reshape(COLS, COLS)
    wait_rows(row_in, rows_s)


def leave_kernel(mixed_ref, sketch_ref, gram_ref, mixed_out, sketch_out, gram_out, sems):
    pairs = ((mixed_ref, mixed_out), (sketch_ref, sketch_out), (gram_ref, gram_out))
    copies = [pltpu.make_async_copy(a, b, sems.at[i]) for i, (a, b) in enumerate(pairs)]
    for copy in copies:
        copy.start()
    for copy in copies:
        copy.wait()


def on_device(panel, flips, picks):
    vmem = pl.BlockSpec(memory_space=pltpu.VMEM)
    hbm = pl.BlockSpec(memory_space=pltpu.HBM)
    dma = pltpu.SemaphoreType.DMA
    f32, i32 = jnp.float32, jnp.int32
    shapes = ((ROWS, COLS), (64, COLS), (COLS, COLS))
    parts = pl.pallas_call(
        kernel,
        out_shape=tuple(pltpu.VMEM(shape, f32) for shape in shapes),
        in_specs=[hbm, hbm, hbm],
        out_specs=(vmem, vmem, vmem),
        scratch_shapes=[
            pltpu.VMEM((ROWS, COLS), f32),
            pltpu.VMEM((ROWS, COLS), f32),
            pltpu.VMEM((DEV, CHUNK, COLS), f32),
            pltpu.VMEM((DEV, CHUNK, COLS), f32),
            pltpu.VMEM((32, 128), i32),
            pltpu.VMEM((64, 128), i32),
            pltpu.VMEM((32, 128), f32),
            pltpu.VMEM((COLS, COLS), f32),
            pltpu.VMEM((64, 128), i32),
            pltpu.SMEM((64, 128), i32),
            pltpu.SMEM((128,), i32),
            pltpu.VMEM((DEV, 2, 1, COLS), f32),
            pltpu.VMEM((DEV, 2, 1, COLS), f32),
            pltpu.VMEM((DEV, 1, COLS), f32),
            pltpu.VMEM((DEV, 1, COLS), f32),
            dma((LOADS,)), dma((3,)), dma((2,)), dma((2,)), dma((2,)), dma((2,)),
            dma, dma, dma, dma,
        ],
        name="sketch",
        compiler_params=pltpu.CompilerParams(
            collective_id=1, has_side_effects=True, vmem_limit_bytes=56 * 2**20
        ),
    )(panel, flips.reshape(32, 128), picks.reshape(64, 128))
    return pl.pallas_call(
        leave_kernel,
        out_shape=tuple(jax.ShapeDtypeStruct(shape, f32) for shape in shapes),
        in_specs=[vmem, vmem, vmem],
        out_specs=(hbm, hbm, hbm),
        scratch_shapes=[dma((3,))],
        name="leave",
    )(*(pltpu.with_memory_space_constraint(p, pltpu.VMEM) for p in parts))


def solution(mesh):
    both = ("narrow", "wide")
    return jax.shard_map(
        on_device,
        mesh=mesh,
        in_specs=(P(both, None), P(both), P()),
        out_specs=(P(both, None), P(both, None), P()),
        check_vma=False,
    )
```

```python
import itertools

import jax
import jax.numpy as jnp
from jax import lax
from jax.experimental import pallas as pl
from jax.experimental.pallas import tpu as pltpu
from jax.sharding import PartitionSpec as P

MESH = pl.DeviceIdType.MESH
DEV = 128
ROWS = 4096
COLS = 128
CHUNK = 32
HALF = 16
LOADS = 4
SCALE = 1.0 / float(ROWS * DEV) ** 0.5


def offsets():
    rest = [o for o in itertools.product(range(4), range(4), range(4), range(2)) if any(o)]
    used = [0] * 6
    order = []

    def load(o):
        out = [0] * 6
        for i in range(3):
            out[2 * i] = (0, 1, 1, 0)[o[i]]
            out[2 * i + 1] = (0, 0, 1, 1)[o[i]]
        return out

    def cost(o):
        total = [u + w for u, w in zip(used, load(o))]
        return -sum(load(o)), max(total) - min(total), max(total)

    while rest:
        best = min(rest, key=cost)
        rest.remove(best)
        order.append(best)
        used = [u + w for u, w in zip(used, load(best))]
    return order


OFFSETS = offsets()
FAR_FIRST = OFFSETS
CROSS = [o for o in OFFSETS if o[3] == 1 and sum(min(v, 4 - v) for v in o[:3]) == 1]
OFFSETS = CROSS + [o for o in OFFSETS if o not in CROSS]


class Place:
    def __init__(self):
        self.narrow, self.wide = lax.axis_index("narrow"), lax.axis_index("wide")
        self.me = self.narrow * 32 + self.wide
        y, z_lo, x = self.wide & 3, (self.wide >> 2) & 1, self.wide >> 3
        core, z = self.narrow & 1, (self.narrow >> 1) * 2 + z_lo
        self.xs = [((x + i) & 3) * 8 for i in range(4)]
        self.ys = [(y + i) & 3 for i in range(4)]
        self.zs = [((z + i) & 1) * 4 for i in range(4)]
        self.zn = [(((z + i) >> 1) & 1) * 2 for i in range(4)]
        self.cs = [core, 1 - core]

    def others(self, offsets=OFFSETS):
        for dx, dy, dz, dc in offsets:
            narrow, wide = self.zn[dz] + self.cs[dc], self.xs[dx] + self.ys[dy] + self.zs[dz]
            yield narrow * 32 + wide, (narrow, wide)


def butterfly(values):
    values = list(values)
    apart = 1
    while apart < len(values):
        for i in range(len(values)):
            if i & apart == 0:
                a, b = values[i], values[i + apart]
                values[i], values[i + apart] = a + b, a - b
        apart *= 2
    return values


def first_pass(x_ref, signs, t_ref, g):
    rows = x_ref[g * 128 : g * 128 + 128, :] * signs[:, g : g + 1]
    out = butterfly([rows[8 * m : 8 * m + 8] for m in range(16)])
    for m in range(16):
        t_ref[g * 128 + 8 * m : g * 128 + 8 * m + 8, :] = out[m]


def second_pass(t_ref):
    def step(g, carry):
        base = (g // 2) * 256 + (g % 2) * 64
        spots = [base + 128 * h + k for h in range(2) for k in range(8)]
        out = butterfly([t_ref[pl.ds(s, 8, stride=8), :] for s in spots])
        for s, value in zip(spots, out):
            t_ref[pl.ds(s, 8, stride=8), :] = value
        return carry

    lax.fori_loop(0, 32, step, 0, unroll=8)


def third_pass(half, t_ref):
    def step(g, carry):
        base = pl.multiple_of((g % 2) * 8 + half * HALF + (g // 2) * CHUNK, 8)
        spots = [base + 256 * m for m in range(16)]
        out = butterfly([t_ref[pl.ds(s, 8), :] for s in spots])
        for s, value in zip(spots, out):
            t_ref[pl.ds(s, 8), :] = value
        return carry

    lax.fori_loop(0, 16, step, 0, unroll=8)


def device_transform(half, src_ref, dst_ref):
    def low(g, carry):
        for u in range(2):
            rows = pl.ds(half * HALF + 8 * u, 8)
            out = butterfly([src_ref[g * 16 + m, rows, :] for m in range(16)])
            for m in range(16):
                dst_ref[g * 16 + m, rows, :] = out[m]
        return carry

    lax.fori_loop(0, 8, low, 0, unroll=2)

    def high(g, carry):
        for u in range(2):
            rows = pl.ds(half * HALF + 8 * u, 8)
            out = butterfly([dst_ref[g + 16 * m, rows, :] for m in range(8)])
            for m in range(8):
                dst_ref[g + 16 * m, rows, :] = out[m] * SCALE
        return carry

    lax.fori_loop(0, 16, high, 0, unroll=4)


def counts_of(me, picks_ref):
    def step(k, total):
        p = picks_ref[pl.ds(k, 1), :]
        here = ((p >> 5) & 127) == me
        q = ((p >> 4) & 1) * (DEV * HALF) + (p >> 12) * HALF + (p & 15)
        hi = jnp.where(here, q >> 7, -1)
        lo = q & 127
        a = (lax.broadcasted_iota(jnp.int32, (32, 128), 0) == hi).astype(jnp.float32)
        b = (lax.broadcasted_iota(jnp.int32, (128, 128), 0) == lo).astype(jnp.float32)
        return total + lax.dot_general(
            a, b, (((1,), (1,)), ((), ())), preferred_element_type=jnp.float32
        )

    return lax.fori_loop(0, 64, step, jnp.zeros((32, 128), jnp.float32))


def kernel(
    panel_ref, flips_hbm, picks_hbm,
    mixed_ref, sketch_ref, gram_ref,
    x_ref, t_ref, in_ref, done_ref, flips_ref, picks_ref, counts_ref, part_ref, wanted_ref, wanted_sm, mine_sm,
    row_out, row_in, gp_out, gp_in,
    load_sem, small_sem, p1s, p1r, p2s, p2r, gps, gpr, rows_s, rows_r,
):
    here = Place()
    me = here.me
    barrier = pltpu.get_barrier_semaphore()
    for _, spot in here.others(FAR_FIRST):
        pl.semaphore_signal(barrier, inc=1, device_id=spot, device_id_type=MESH)
    small = [
        pltpu.make_async_copy(flips_hbm, flips_ref, small_sem.at[0]),
        pltpu.make_async_copy(picks_hbm, picks_ref, small_sem.at[1]),
        pltpu.make_async_copy(picks_hbm.at[me >> 1], mine_sm, small_sem.at[2]),
    ]
    small[0].start()
    loads = []
    for i in range(LOADS):
        rows = pl.ds(i * (ROWS // LOADS), ROWS // LOADS)
        loads.append(pltpu.make_async_copy(panel_ref.at[rows], x_ref.at[rows], load_sem.at[i]))
        loads[-1].start()
    small[1].start()
    small[2].start()
    small[0].wait()
    signs = (1 - 2 * flips_ref[...]).astype(jnp.float32).T
    for g in range(32):
        if g % (32 // LOADS) == 0:
            loads[g // (32 // LOADS)].wait()
        first_pass(x_ref, signs, t_ref, g)
    second_pass(t_ref)
    third_pass(0, t_ref)
    pl.semaphore_wait(barrier, DEV - 1)

    def rows_of(d, half):
        return pl.ds(pl.multiple_of(d * CHUNK + half * HALF, HALF), HALF)

    def send(src, dst, send_sem, recv_sem, spot):
        pltpu.make_async_remote_copy(
            src, dst, send_sem, recv_sem, device_id=spot, device_id_type=MESH
        ).start()

    def send_in(half):
        part = pl.ds(half * HALF, HALF)
        for d, spot in here.others():
            send(t_ref.at[rows_of(d, half)], in_ref.at[me, part], p1s.at[half], p1r.at[half], spot)

    def send_back(half):
        part = pl.ds(half * HALF, HALF)
        for d, spot in here.others():
            send(done_ref.at[d, part], mixed_ref.at[rows_of(me, half)], p2s.at[half], p2r.at[half], spot)

    def wait_bytes(sem):
        others = pl.ds(0, (DEV - 1) * HALF)
        pltpu.make_async_copy(x_ref.at[others], t_ref.at[others], sem).wait()

    def wait_rows(ref, sem):
        pltpu.make_async_copy(ref.at[pl.ds(0, DEV - 1)], ref.at[pl.ds(0, DEV - 1)], sem).wait()

    def add_gram(half):
        def step(g, total):
            rows = done_ref[pl.ds(g * 8, 8), pl.ds(half * HALF, HALF), :].reshape(128, COLS)
            left = rows.T * counts_ref[pl.ds(half * 16 + g, 1), :]
            return total + jnp.dot(
                left, rows, precision=lax.Precision.HIGHEST, preferred_element_type=jnp.float32
            )

        part_ref[...] = lax.fori_loop(0, 16, step, part_ref[...], unroll=4)

    send_in(0)
    third_pass(1, t_ref)
    send_in(1)
    in_ref[me] = t_ref[pl.ds(pl.multiple_of(me * CHUNK, CHUNK), CHUNK), :]

    small[1].wait()
    p = picks_ref[...]
    lane = lax.broadcasted_iota(jnp.int32, p.shape, 1)
    local = jnp.where((p >> 12) == me, p & (ROWS - 1), 0)
    even = jnp.max(jnp.where(lane < 64, local, 0), axis=1, keepdims=True)
    odd = jnp.max(jnp.where(lane < 64, 0, local), axis=1, keepdims=True)
    wanted_ref[...] = jnp.where(lane == 0, even, odd)
    wanted = pltpu.make_async_copy(wanted_ref, wanted_sm, small_sem.at[1])
    wanted.start()
    counts_ref[...] = counts_of(me, picks_ref)
    part_ref[...] = jnp.zeros_like(part_ref)

    wait_bytes(p1r.at[0])
    device_transform(0, in_ref, done_ref)
    send_back(0)
    add_gram(0)
    wait_bytes(p1r.at[1])
    device_transform(1, in_ref, done_ref)
    add_gram(1)
    gp_out[...] = part_ref[...].reshape(DEV, 1, COLS)
    for d, spot in here.others():
        send(gp_out.at[d], gp_in.at[me], gps, gpr, spot)
    send_back(1)
    gp_in[me] = gp_out[me]
    mixed_ref[pl.ds(pl.multiple_of(me * CHUNK, CHUNK), CHUNK), :] = done_ref[me]
    wait_rows(gp_in, gpr)
    gram_row = jnp.sum(gp_in[...], axis=0, keepdims=True) * (1.0 / 8192.0)
    row_out[:, 1] = jnp.broadcast_to(gram_row, (DEV, 1, COLS))

    wanted.wait()
    wait_bytes(p2r.at[0])
    wait_bytes(p2r.at[1])

    def gather(k, carry):
        for j in range(2):
            row_out[2 * k + j, 0] = mixed_ref[pl.ds(wanted_sm[k, j], 1), :]
        return carry

    lax.fori_loop(0, DEV // 2, gather, 0, unroll=8)
    for d, spot in here.others():
        send(row_out.at[d], row_in.at[me], rows_s, rows_r, spot)
    row_in[me] = row_out[me]
    small[2].wait()
    for half in range(2):
        wait_bytes(p1s.at[half])
        wait_bytes(p2s.at[half])
    wait_rows(gp_in, gps)
    wait_rows(row_in, rows_r)
    start = (me & 1) * 64

    def pick_row(i, carry):
        sketch_ref[pl.ds(i, 1), :] = row_in[(mine_sm[start + i] >> 12) & (DEV - 1), 0]
        return carry

    lax.fori_loop(0, 64, pick_row, 0, unroll=16)
    gram_ref[...] = row_in[:, 1].reshape(COLS, COLS)
    wait_rows(row_in, rows_s)


def leave_kernel(mixed_ref, sketch_ref, gram_ref, mixed_out, sketch_out, gram_out, sems):
    pairs = ((mixed_ref, mixed_out), (sketch_ref, sketch_out), (gram_ref, gram_out))
    copies = [pltpu.make_async_copy(a, b, sems.at[i]) for i, (a, b) in enumerate(pairs)]
    for copy in copies:
        copy.start()
    for copy in copies:
        copy.wait()


def on_device(panel, flips, picks):
    vmem = pl.BlockSpec(memory_space=pltpu.VMEM)
    hbm = pl.BlockSpec(memory_space=pltpu.HBM)
    dma = pltpu.SemaphoreType.DMA
    f32, i32 = jnp.float32, jnp.int32
    shapes = ((ROWS, COLS), (64, COLS), (COLS, COLS))
    parts = pl.pallas_call(
        kernel,
        out_shape=tuple(pltpu.VMEM(shape, f32) for shape in shapes),
        in_specs=[hbm, hbm, hbm],
        out_specs=(vmem, vmem, vmem),
        scratch_shapes=[
            pltpu.VMEM((ROWS, COLS), f32),
            pltpu.VMEM((ROWS, COLS), f32),
            pltpu.VMEM((DEV, CHUNK, COLS), f32),
            pltpu.VMEM((DEV, CHUNK, COLS), f32),
            pltpu.VMEM((32, 128), i32),
            pltpu.VMEM((64, 128), i32),
            pltpu.VMEM((32, 128), f32),
            pltpu.VMEM((COLS, COLS), f32),
            pltpu.VMEM((64, 128), i32),
            pltpu.SMEM((64, 128), i32),
            pltpu.SMEM((128,), i32),
            pltpu.VMEM((DEV, 2, 1, COLS), f32),
            pltpu.VMEM((DEV, 2, 1, COLS), f32),
            pltpu.VMEM((DEV, 1, COLS), f32),
            pltpu.VMEM((DEV, 1, COLS), f32),
            dma((LOADS,)), dma((3,)), dma((2,)), dma((2,)), dma((2,)), dma((2,)),
            dma, dma, dma, dma,
        ],
        name="sketch",
        compiler_params=pltpu.CompilerParams(
            collective_id=1, has_side_effects=True, vmem_limit_bytes=56 * 2**20
        ),
    )(panel, flips.reshape(32, 128), picks.reshape(64, 128))
    return pl.pallas_call(
        leave_kernel,
        out_shape=tuple(jax.ShapeDtypeStruct(shape, f32) for shape in shapes),
        in_specs=[vmem, vmem, vmem],
        out_specs=(hbm, hbm, hbm),
        scratch_shapes=[dma((3,))],
        name="leave",
    )(*(pltpu.with_memory_space_constraint(p, pltpu.VMEM) for p in parts))


def solution(mesh):
    both = ("narrow", "wide")
    return jax.shard_map(
        on_device,
        mesh=mesh,
        in_specs=(P(both, None), P(both), P()),
        out_specs=(P(both, None), P(both, None), P()),
        check_vma=False,
    )
```

```python
import itertools

import jax
import jax.numpy as jnp
from jax import lax
from jax.experimental import pallas as pl
from jax.experimental.pallas import tpu as pltpu
from jax.sharding import PartitionSpec as P

MESH = pl.DeviceIdType.MESH
DEV = 128
ROWS = 4096
COLS = 128
CHUNK = 32
HALF = 16
LOADS = 4
SCALE = 1.0 / float(ROWS * DEV) ** 0.5


def offsets():
    rest = [o for o in itertools.product(range(4), range(4), range(4), range(2)) if any(o)]
    used = [0] * 6
    order = []

    def load(o):
        out = [0] * 6
        for i in range(3):
            out[2 * i] = (0, 1, 1, 0)[o[i]]
            out[2 * i + 1] = (0, 0, 1, 1)[o[i]]
        return out

    def cost(o):
        total = [u + w for u, w in zip(used, load(o))]
        return -sum(load(o)), max(total) - min(total), max(total)

    while rest:
        best = min(rest, key=cost)
        rest.remove(best)
        order.append(best)
        used = [u + w for u, w in zip(used, load(best))]
    return order


OFFSETS = offsets()
FAR_FIRST = OFFSETS
CROSS = [o for o in OFFSETS if o[3] == 1 and sum(min(v, 4 - v) for v in o[:3]) == 1]
OFFSETS = CROSS + [o for o in OFFSETS if o not in CROSS]
NEAR = [o for o in FAR_FIRST if 1 <= sum(min(v, 4 - v) for v in o[:3]) <= 3]
DIRECT = [o for o in FAR_FIRST if o not in NEAR or o[3] == 0]
PASSED_ON = [o for o in NEAR if o[3] == 0]


class Place:
    def __init__(self):
        self.narrow, self.wide = lax.axis_index("narrow"), lax.axis_index("wide")
        self.me = self.narrow * 32 + self.wide
        y, z_lo, x = self.wide & 3, (self.wide >> 2) & 1, self.wide >> 3
        core, z = self.narrow & 1, (self.narrow >> 1) * 2 + z_lo
        self.xs = [((x + i) & 3) * 8 for i in range(4)]
        self.ys = [(y + i) & 3 for i in range(4)]
        self.zs = [((z + i) & 1) * 4 for i in range(4)]
        self.zn = [(((z + i) >> 1) & 1) * 2 for i in range(4)]
        self.cs = [core, 1 - core]
        self.core, self.twin = core, (self.narrow ^ 1, self.wide)

    def others(self, offsets=OFFSETS):
        for dx, dy, dz, dc in offsets:
            narrow, wide = self.zn[dz] + self.cs[dc], self.xs[dx] + self.ys[dy] + self.zs[dz]
            yield narrow * 32 + wide, (narrow, wide)


def butterfly(values):
    values = list(values)
    apart = 1
    while apart < len(values):
        for i in range(len(values)):
            if i & apart == 0:
                a, b = values[i], values[i + apart]
                values[i], values[i + apart] = a + b, a - b
        apart *= 2
    return values


def first_pass(x_ref, signs, t_ref, g):
    rows = x_ref[g * 128 : g * 128 + 128, :] * signs[:, g : g + 1]
    out = butterfly([rows[8 * m : 8 * m + 8] for m in range(16)])
    for m in range(16):
        t_ref[g * 128 + 8 * m : g * 128 + 8 * m + 8, :] = out[m]


def second_pass(t_ref):
    def step(g, carry):
        base = (g // 2) * 256 + (g % 2) * 64
        spots = [base + 128 * h + k for h in range(2) for k in range(8)]
        out = butterfly([t_ref[pl.ds(s, 8, stride=8), :] for s in spots])
        for s, value in zip(spots, out):
            t_ref[pl.ds(s, 8, stride=8), :] = value
        return carry

    lax.fori_loop(0, 32, step, 0, unroll=8)


def third_pass(half, t_ref):
    def step(g, carry):
        base = pl.multiple_of((g % 2) * 8 + half * HALF + (g // 2) * CHUNK, 8)
        spots = [base + 256 * m for m in range(16)]
        out = butterfly([t_ref[pl.ds(s, 8), :] for s in spots])
        for s, value in zip(spots, out):
            t_ref[pl.ds(s, 8), :] = value
        return carry

    lax.fori_loop(0, 16, step, 0, unroll=8)


def device_transform(half, src_ref, dst_ref):
    def low(g, carry):
        for u in range(2):
            rows = pl.ds(half * HALF + 8 * u, 8)
            out = butterfly([src_ref[g * 16 + m, rows, :] for m in range(16)])
            for m in range(16):
                dst_ref[g * 16 + m, rows, :] = out[m]
        return carry

    lax.fori_loop(0, 8, low, 0, unroll=2)

    def high(g, carry):
        for u in range(2):
            rows = pl.ds(half * HALF + 8 * u, 8)
            out = butterfly([dst_ref[g + 16 * m, rows, :] for m in range(8)])
            for m in range(8):
                dst_ref[g + 16 * m, rows, :] = out[m] * SCALE
        return carry

    lax.fori_loop(0, 16, high, 0, unroll=4)


def counts_of(me, picks_ref):
    def step(k, total):
        p = picks_ref[pl.ds(k, 1), :]
        here = ((p >> 5) & 127) == me
        q = ((p >> 4) & 1) * (DEV * HALF) + (p >> 12) * HALF + (p & 15)
        hi = jnp.where(here, q >> 7, -1)
        lo = q & 127
        a = (lax.broadcasted_iota(jnp.int32, (32, 128), 0) == hi).astype(jnp.float32)
        b = (lax.broadcasted_iota(jnp.int32, (128, 128), 0) == lo).astype(jnp.float32)
        return total + lax.dot_general(
            a, b, (((1,), (1,)), ((), ())), preferred_element_type=jnp.float32
        )

    return lax.fori_loop(0, 64, step, jnp.zeros((32, 128), jnp.float32))


def kernel(
    panel_ref, flips_hbm, picks_hbm,
    mixed_ref, sketch_ref, gram_ref,
    x_ref, t_ref, in_ref, done_ref, flips_ref, picks_ref, counts_ref, part_ref, wanted_ref, wanted_sm, mine_sm,
    row_out, row_in, passed, gp_out, gp_in,
    load_sem, small_sem, p1s, p1r, p2s, p2r, gps, gpr, rows_s, rows_r, fws, fwr,
):
    here = Place()
    me = here.me
    barrier = pltpu.get_barrier_semaphore()
    for _, spot in here.others(FAR_FIRST):
        pl.semaphore_signal(barrier, inc=1, device_id=spot, device_id_type=MESH)
    small = [
        pltpu.make_async_copy(flips_hbm, flips_ref, small_sem.at[0]),
        pltpu.make_async_copy(picks_hbm, picks_ref, small_sem.at[1]),
        pltpu.make_async_copy(picks_hbm.at[me >> 1], mine_sm, small_sem.at[2]),
    ]
    small[0].start()
    loads = []
    for i in range(LOADS):
        rows = pl.ds(i * (ROWS // LOADS), ROWS // LOADS)
        loads.append(pltpu.make_async_copy(panel_ref.at[rows], x_ref.at[rows], load_sem.at[i]))
        loads[-1].start()
    small[1].start()
    small[2].start()
    small[0].wait()
    signs = (1 - 2 * flips_ref[...]).astype(jnp.float32).T
    for g in range(32):
        if g % (32 // LOADS) == 0:
            loads[g // (32 // LOADS)].wait()
        first_pass(x_ref, signs, t_ref, g)
    second_pass(t_ref)
    third_pass(0, t_ref)
    pl.semaphore_wait(barrier, DEV - 1)

    def rows_of(d, half):
        return pl.ds(pl.multiple_of(d * CHUNK + half * HALF, HALF), HALF)

    def send(src, dst, send_sem, recv_sem, spot):
        pltpu.make_async_remote_copy(
            src, dst, send_sem, recv_sem, device_id=spot, device_id_type=MESH
        ).start()

    def send_in(half):
        part = pl.ds(half * HALF, HALF)
        for d, spot in here.others():
            send(t_ref.at[rows_of(d, half)], in_ref.at[me, part], p1s.at[half], p1r.at[half], spot)

    def send_back(half):
        part = pl.ds(half * HALF, HALF)
        for d, spot in here.others():
            send(done_ref.at[d, part], mixed_ref.at[rows_of(me, half)], p2s.at[half], p2r.at[half], spot)

    def wait_bytes(sem):
        others = pl.ds(0, (DEV - 1) * HALF)
        pltpu.make_async_copy(x_ref.at[others], t_ref.at[others], sem).wait()

    def wait_rows(ref, sem):
        pltpu.make_async_copy(ref.at[pl.ds(0, DEV - 1)], ref.at[pl.ds(0, DEV - 1)], sem).wait()

    def add_gram(half):
        def step(g, total):
            rows = done_ref[pl.ds(g * 8, 8), pl.ds(half * HALF, HALF), :].reshape(128, COLS)
            left = rows.T * counts_ref[pl.ds(half * 16 + g, 1), :]
            return total + jnp.dot(
                left, rows, precision=lax.Precision.HIGHEST, preferred_element_type=jnp.float32
            )

        part_ref[...] = lax.fori_loop(0, 16, step, part_ref[...], unroll=4)

    send_in(0)
    third_pass(1, t_ref)
    send_in(1)
    in_ref[me] = t_ref[pl.ds(pl.multiple_of(me * CHUNK, CHUNK), CHUNK), :]

    small[1].wait()
    p = picks_ref[...]
    lane = lax.broadcasted_iota(jnp.int32, p.shape, 1)
    local = jnp.where((p >> 12) == me, p & (ROWS - 1), 0)
    even = jnp.max(jnp.where(lane < 64, local, 0), axis=1, keepdims=True)
    odd = jnp.max(jnp.where(lane < 64, 0, local), axis=1, keepdims=True)
    wanted_ref[...] = jnp.where(lane == 0, even, odd)
    wanted = pltpu.make_async_copy(wanted_ref, wanted_sm, small_sem.at[1])
    wanted.start()
    counts_ref[...] = counts_of(me, picks_ref)
    part_ref[...] = jnp.zeros_like(part_ref)

    wait_bytes(p1r.at[0])
    device_transform(0, in_ref, done_ref)
    send_back(0)
    add_gram(0)
    wait_bytes(p1r.at[1])
    device_transform(1, in_ref, done_ref)
    add_gram(1)
    gp_out[...] = part_ref[...].reshape(DEV, 1, COLS)
    for d, spot in here.others():
        send(gp_out.at[d], gp_in.at[me], gps, gpr, spot)
    send_back(1)
    gp_in[me] = gp_out[me]
    mixed_ref[pl.ds(pl.multiple_of(me * CHUNK, CHUNK), CHUNK), :] = done_ref[me]
    wait_rows(gp_in, gpr)
    gram_row = jnp.sum(gp_in[...], axis=0, keepdims=True) * (1.0 / 8192.0)
    row_out[:, 1] = jnp.broadcast_to(gram_row, (DEV, 1, COLS))

    wanted.wait()
    wait_bytes(p2r.at[0])
    wait_bytes(p2r.at[1])

    def gather(k, carry):
        for j in range(2):
            row_out[2 * k + j, 0] = mixed_ref[pl.ds(wanted_sm[k, j], 1), :]
        return carry

    lax.fori_loop(0, DEV // 2, gather, 0, unroll=8)
    swaps = []
    for side in range(2):
        block = pl.ds(pl.multiple_of(side * 64 + (1 - here.core) * 32, 32), 32)
        swaps.append(
            pltpu.make_async_remote_copy(
                row_out.at[block], passed.at[side], fws.at[side], fwr.at[side],
                device_id=here.twin, device_id_type=MESH,
            )
        )
        swaps[-1].start()
    for d, spot in here.others(DIRECT):
        send(row_out.at[d], row_in.at[me], rows_s, rows_r, spot)
    for swap in swaps:
        swap.wait()
    for _, (narrow, wide) in here.others(PASSED_ON):
        send(passed.at[narrow >> 1, wide], row_in.at[me ^ 32], rows_s, rows_r, (narrow, wide))
    row_in[me] = row_out[me]
    small[2].wait()
    for half in range(2):
        wait_bytes(p1s.at[half])
        wait_bytes(p2s.at[half])
    wait_rows(gp_in, gps)
    wait_rows(row_in, rows_r)
    start = (me & 1) * 64

    def pick_row(i, carry):
        sketch_ref[pl.ds(i, 1), :] = row_in[(mine_sm[start + i] >> 12) & (DEV - 1), 0]
        return carry

    lax.fori_loop(0, 64, pick_row, 0, unroll=16)
    gram_ref[...] = row_in[:, 1].reshape(COLS, COLS)
    wait_rows(row_in, rows_s)


def leave_kernel(mixed_ref, sketch_ref, gram_ref, mixed_out, sketch_out, gram_out, sems):
    pairs = ((mixed_ref, mixed_out), (sketch_ref, sketch_out), (gram_ref, gram_out))
    copies = [pltpu.make_async_copy(a, b, sems.at[i]) for i, (a, b) in enumerate(pairs)]
    for copy in copies:
        copy.start()
    for copy in copies:
        copy.wait()


def on_device(panel, flips, picks):
    vmem = pl.BlockSpec(memory_space=pltpu.VMEM)
    hbm = pl.BlockSpec(memory_space=pltpu.HBM)
    dma = pltpu.SemaphoreType.DMA
    f32, i32 = jnp.float32, jnp.int32
    shapes = ((ROWS, COLS), (64, COLS), (COLS, COLS))
    parts = pl.pallas_call(
        kernel,
        out_shape=tuple(pltpu.VMEM(shape, f32) for shape in shapes),
        in_specs=[hbm, hbm, hbm],
        out_specs=(vmem, vmem, vmem),
        scratch_shapes=[
            pltpu.VMEM((ROWS, COLS), f32),
            pltpu.VMEM((ROWS, COLS), f32),
            pltpu.VMEM((DEV, CHUNK, COLS), f32),
            pltpu.VMEM((DEV, CHUNK, COLS), f32),
            pltpu.VMEM((32, 128), i32),
            pltpu.VMEM((64, 128), i32),
            pltpu.VMEM((32, 128), f32),
            pltpu.VMEM((COLS, COLS), f32),
            pltpu.VMEM((64, 128), i32),
            pltpu.SMEM((64, 128), i32),
            pltpu.SMEM((128,), i32),
            pltpu.VMEM((DEV, 2, 1, COLS), f32),
            pltpu.VMEM((DEV, 2, 1, COLS), f32),
            pltpu.VMEM((2, 32, 2, 1, COLS), f32),
            pltpu.VMEM((DEV, 1, COLS), f32),
            pltpu.VMEM((DEV, 1, COLS), f32),
            dma((LOADS,)), dma((3,)), dma((2,)), dma((2,)), dma((2,)), dma((2,)),
            dma, dma, dma, dma, dma((2,)), dma((2,)),
        ],
        name="sketch",
        compiler_params=pltpu.CompilerParams(
            collective_id=1, has_side_effects=True, vmem_limit_bytes=56 * 2**20
        ),
    )(panel, flips.reshape(32, 128), picks.reshape(64, 128))
    return pl.pallas_call(
        leave_kernel,
        out_shape=tuple(jax.ShapeDtypeStruct(shape, f32) for shape in shapes),
        in_specs=[vmem, vmem, vmem],
        out_specs=(hbm, hbm, hbm),
        scratch_shapes=[dma((3,))],
        name="leave",
    )(*(pltpu.with_memory_space_constraint(p, pltpu.VMEM) for p in parts))


def solution(mesh):
    both = ("narrow", "wide")
    return jax.shard_map(
        on_device,
        mesh=mesh,
        in_specs=(P(both, None), P(both), P()),
        out_specs=(P(both, None), P(both, None), P()),
        check_vma=False,
    )
```

```python
import itertools

import jax
import jax.numpy as jnp
from jax import lax
from jax.experimental import pallas as pl
from jax.experimental.pallas import tpu as pltpu
from jax.sharding import PartitionSpec as P

MESH = pl.DeviceIdType.MESH
DEV = 128
ROWS = 4096
COLS = 128
CHUNK = 32
HALF = 16
LOADS = 4
SCALE = 1.0 / float(ROWS * DEV) ** 0.5


def offsets():
    rest = [o for o in itertools.product(range(4), range(4), range(4), range(2)) if any(o)]
    used = [0] * 6
    order = []

    def load(o):
        out = [0] * 6
        for i in range(3):
            out[2 * i] = (0, 1, 1, 0)[o[i]]
            out[2 * i + 1] = (0, 0, 1, 1)[o[i]]
        return out

    def cost(o):
        total = [u + w for u, w in zip(used, load(o))]
        return -sum(load(o)), max(total) - min(total), max(total)

    while rest:
        best = min(rest, key=cost)
        rest.remove(best)
        order.append(best)
        used = [u + w for u, w in zip(used, load(best))]
    return order


OFFSETS = offsets()
FAR_FIRST = OFFSETS
CROSS = [o for o in OFFSETS if o[3] == 1 and sum(min(v, 4 - v) for v in o[:3]) == 1]
OFFSETS = CROSS + [o for o in OFFSETS if o not in CROSS]
SAME_CORE = [o for o in OFFSETS if o[3] == 0]


class Place:
    def __init__(self):
        self.narrow, self.wide = lax.axis_index("narrow"), lax.axis_index("wide")
        self.me = self.narrow * 32 + self.wide
        y, z_lo, x = self.wide & 3, (self.wide >> 2) & 1, self.wide >> 3
        core, z = self.narrow & 1, (self.narrow >> 1) * 2 + z_lo
        self.xs = [((x + i) & 3) * 8 for i in range(4)]
        self.ys = [(y + i) & 3 for i in range(4)]
        self.zs = [((z + i) & 1) * 4 for i in range(4)]
        self.zn = [(((z + i) >> 1) & 1) * 2 for i in range(4)]
        self.cs = [core, 1 - core]
        self.side = self.narrow >> 1

    def others(self, offsets=OFFSETS):
        for dx, dy, dz, dc in offsets:
            narrow, wide = self.zn[dz] + self.cs[dc], self.xs[dx] + self.ys[dy] + self.zs[dz]
            yield narrow * 32 + wide, (narrow, wide)


def butterfly(values):
    values = list(values)
    apart = 1
    while apart < len(values):
        for i in range(len(values)):
            if i & apart == 0:
                a, b = values[i], values[i + apart]
                values[i], values[i + apart] = a + b, a - b
        apart *= 2
    return values


def first_pass(x_ref, signs, t_ref, g):
    rows = x_ref[g * 128 : g * 128 + 128, :] * signs[:, g : g + 1]
    out = butterfly([rows[8 * m : 8 * m + 8] for m in range(16)])
    for m in range(16):
        t_ref[g * 128 + 8 * m : g * 128 + 8 * m + 8, :] = out[m]


def second_pass(t_ref):
    def step(g, carry):
        base = (g // 2) * 256 + (g % 2) * 64
        spots = [base + 128 * h + k for h in range(2) for k in range(8)]
        out = butterfly([t_ref[pl.ds(s, 8, stride=8), :] for s in spots])
        for s, value in zip(spots, out):
            t_ref[pl.ds(s, 8, stride=8), :] = value
        return carry

    lax.fori_loop(0, 32, step, 0, unroll=8)


def third_pass(half, t_ref):
    def step(g, carry):
        base = pl.multiple_of((g % 2) * 8 + half * HALF + (g // 2) * CHUNK, 8)
        spots = [base + 256 * m for m in range(16)]
        out = butterfly([t_ref[pl.ds(s, 8), :] for s in spots])
        for s, value in zip(spots, out):
            t_ref[pl.ds(s, 8), :] = value
        return carry

    lax.fori_loop(0, 16, step, 0, unroll=8)


def device_transform(half, src_ref, dst_ref):
    def low(g, carry):
        for u in range(2):
            rows = pl.ds(half * HALF + 8 * u, 8)
            out = butterfly([src_ref[g * 16 + m, rows, :] for m in range(16)])
            for m in range(16):
                dst_ref[g * 16 + m, rows, :] = out[m]
        return carry

    lax.fori_loop(0, 8, low, 0, unroll=2)

    def high(g, carry):
        for u in range(2):
            rows = pl.ds(half * HALF + 8 * u, 8)
            out = butterfly([dst_ref[g + 16 * m, rows, :] for m in range(8)])
            for m in range(8):
                dst_ref[g + 16 * m, rows, :] = out[m] * SCALE
        return carry

    lax.fori_loop(0, 16, high, 0, unroll=4)


def counts_of(me, picks_ref):
    def step(k, total):
        p = picks_ref[pl.ds(k, 1), :]
        here = ((p >> 5) & 127) == me
        q = ((p >> 4) & 1) * (DEV * HALF) + (p >> 12) * HALF + (p & 15)
        hi = jnp.where(here, q >> 7, -1)
        lo = q & 127
        a = (lax.broadcasted_iota(jnp.int32, (32, 128), 0) == hi).astype(jnp.float32)
        b = (lax.broadcasted_iota(jnp.int32, (128, 128), 0) == lo).astype(jnp.float32)
        return total + lax.dot_general(
            a, b, (((1,), (1,)), ((), ())), preferred_element_type=jnp.float32
        )

    return lax.fori_loop(0, 64, step, jnp.zeros((32, 128), jnp.float32))


def kernel(
    panel_ref, flips_hbm, picks_hbm,
    mixed_ref, sketch_ref, gram_ref,
    x_ref, t_ref, in_ref, done_ref, flips_ref, picks_ref, counts_ref, part_ref, wanted_ref, wanted_sm, mine_sm,
    row_out, row_in, gp_out, gp_in,
    load_sem, small_sem, p1s, p1r, p2s, p2r, gps, gpr, rows_s, rows_r,
):
    here = Place()
    me = here.me
    barrier = pltpu.get_barrier_semaphore()
    for _, spot in here.others(FAR_FIRST):
        pl.semaphore_signal(barrier, inc=1, device_id=spot, device_id_type=MESH)
    small = [
        pltpu.make_async_copy(flips_hbm, flips_ref, small_sem.at[0]),
        pltpu.make_async_copy(picks_hbm, picks_ref, small_sem.at[1]),
        pltpu.make_async_copy(picks_hbm.at[me >> 1], mine_sm, small_sem.at[2]),
    ]
    small[0].start()
    loads = []
    for i in range(LOADS):
        rows = pl.ds(i * (ROWS // LOADS), ROWS // LOADS)
        loads.append(pltpu.make_async_copy(panel_ref.at[rows], x_ref.at[rows], load_sem.at[i]))
        loads[-1].start()
    small[1].start()
    small[2].start()
    small[0].wait()
    signs = (1 - 2 * flips_ref[...]).astype(jnp.float32).T
    for g in range(32):
        if g % (32 // LOADS) == 0:
            loads[g // (32 // LOADS)].wait()
        first_pass(x_ref, signs, t_ref, g)
    second_pass(t_ref)
    third_pass(0, t_ref)
    pl.semaphore_wait(barrier, DEV - 1)

    def rows_of(d, half):
        return pl.ds(pl.multiple_of(d * CHUNK + half * HALF, HALF), HALF)

    def send(src, dst, send_sem, recv_sem, spot):
        pltpu.make_async_remote_copy(
            src, dst, send_sem, recv_sem, device_id=spot, device_id_type=MESH
        ).start()

    def send_in(half):
        part = pl.ds(half * HALF, HALF)
        for d, spot in here.others():
            send(t_ref.at[rows_of(d, half)], in_ref.at[me, part], p1s.at[half], p1r.at[half], spot)

    def send_back(half):
        part = pl.ds(half * HALF, HALF)
        for d, spot in here.others():
            send(done_ref.at[d, part], mixed_ref.at[rows_of(me, half)], p2s.at[half], p2r.at[half], spot)

    def wait_bytes(sem):
        others = pl.ds(0, (DEV - 1) * HALF)
        pltpu.make_async_copy(x_ref.at[others], t_ref.at[others], sem).wait()

    def wait_rows(ref, sem):
        pltpu.make_async_copy(ref.at[pl.ds(0, DEV - 1)], ref.at[pl.ds(0, DEV - 1)], sem).wait()

    def wait_sums(sem):
        rows = row_in.at[pl.ds(0, 42)]
        pltpu.make_async_copy(rows, rows, sem).wait()

    def add_gram(half):
        def step(g, total):
            rows = done_ref[pl.ds(g * 8, 8), pl.ds(half * HALF, HALF), :].reshape(128, COLS)
            left = rows.T * counts_ref[pl.ds(half * 16 + g, 1), :]
            return total + jnp.dot(
                left, rows, precision=lax.Precision.HIGHEST, preferred_element_type=jnp.float32
            )

        part_ref[...] = lax.fori_loop(0, 16, step, part_ref[...], unroll=4)

    send_in(0)
    third_pass(1, t_ref)
    send_in(1)
    in_ref[me] = t_ref[pl.ds(pl.multiple_of(me * CHUNK, CHUNK), CHUNK), :]

    small[1].wait()
    p = picks_ref[...]
    lane = lax.broadcasted_iota(jnp.int32, p.shape, 1)
    local = jnp.where((p >> 12) == me, p & (ROWS - 1), 0)
    even = jnp.max(jnp.where(lane < 64, local, 0), axis=1, keepdims=True)
    odd = jnp.max(jnp.where(lane < 64, 0, local), axis=1, keepdims=True)
    wanted_ref[...] = jnp.where(lane == 0, even, odd)
    wanted = pltpu.make_async_copy(wanted_ref, wanted_sm, small_sem.at[1])
    wanted.start()
    counts_ref[...] = counts_of(me, picks_ref)
    part_ref[...] = jnp.zeros_like(part_ref)

    wait_bytes(p1r.at[0])
    device_transform(0, in_ref, done_ref)
    send_back(0)
    add_gram(0)
    wait_bytes(p1r.at[1])
    device_transform(1, in_ref, done_ref)
    add_gram(1)
    for core in range(2):
        for side in range(2):
            rows = pl.ds((2 * side + core) * 32, 32)
            gp_out[side, :, core] = part_ref[rows, :].reshape(32, 1, COLS)
    for _, (narrow, wide) in here.others(SAME_CORE):
        send(gp_out.at[narrow >> 1, wide], gp_in.at[here.side, here.wide], gps, gpr, (narrow, wide))
    send_back(1)
    gp_in[here.side, here.wide] = gp_out[here.side, here.wide]
    mixed_ref[pl.ds(pl.multiple_of(me * CHUNK, CHUNK), CHUNK), :] = done_ref[me]
    wait_sums(gpr)
    sums = jnp.sum(gp_in[...], axis=(0, 1)) * (1.0 / 8192.0)
    for core in range(2):
        row_out[:, 1 + core] = jnp.broadcast_to(sums[core : core + 1], (DEV, 1, COLS))

    wanted.wait()
    wait_bytes(p2r.at[0])
    wait_bytes(p2r.at[1])

    def gather(k, carry):
        for j in range(2):
            row_out[2 * k + j, 0] = mixed_ref[pl.ds(wanted_sm[k, j], 1), :]
        return carry

    lax.fori_loop(0, DEV // 2, gather, 0, unroll=8)
    for d, spot in here.others():
        send(row_out.at[d], row_in.at[me], rows_s, rows_r, spot)
    row_in[me] = row_out[me]
    small[2].wait()
    for half in range(2):
        wait_bytes(p1s.at[half])
        wait_bytes(p2s.at[half])
    wait_sums(gps)
    wait_rows(row_in, rows_r)
    start = (me & 1) * 64

    def pick_row(i, carry):
        sketch_ref[pl.ds(i, 1), :] = row_in[(mine_sm[start + i] >> 12) & (DEV - 1), 0]
        return carry

    lax.fori_loop(0, 64, pick_row, 0, unroll=16)
    for side in range(2):
        for core in range(2):
            first, second = (row_in[pl.ds(side * 64 + 32 * c, 32), 1 + core] for c in range(2))
            gram_ref[pl.ds(side * 64 + 32 * core, 32), :] = (first + second).reshape(32, COLS)
    wait_rows(row_in, rows_s)


def leave_kernel(mixed_ref, sketch_ref, gram_ref, mixed_out, sketch_out, gram_out, sems):
    pairs = ((mixed_ref, mixed_out), (sketch_ref, sketch_out), (gram_ref, gram_out))
    copies = [pltpu.make_async_copy(a, b, sems.at[i]) for i, (a, b) in enumerate(pairs)]
    for copy in copies:
        copy.start()
    for copy in copies:
        copy.wait()


def on_device(panel, flips, picks):
    vmem = pl.BlockSpec(memory_space=pltpu.VMEM)
    hbm = pl.BlockSpec(memory_space=pltpu.HBM)
    dma = pltpu.SemaphoreType.DMA
    f32, i32 = jnp.float32, jnp.int32
    shapes = ((ROWS, COLS), (64, COLS), (COLS, COLS))
    parts = pl.pallas_call(
        kernel,
        out_shape=tuple(pltpu.VMEM(shape, f32) for shape in shapes),
        in_specs=[hbm, hbm, hbm],
        out_specs=(vmem, vmem, vmem),
        scratch_shapes=[
            pltpu.VMEM((ROWS, COLS), f32),
            pltpu.VMEM((ROWS, COLS), f32),
            pltpu.VMEM((DEV, CHUNK, COLS), f32),
            pltpu.VMEM((DEV, CHUNK, COLS), f32),
            pltpu.VMEM((32, 128), i32),
            pltpu.VMEM((64, 128), i32),
            pltpu.VMEM((32, 128), f32),
            pltpu.VMEM((COLS, COLS), f32),
            pltpu.VMEM((64, 128), i32),
            pltpu.SMEM((64, 128), i32),
            pltpu.SMEM((128,), i32),
            pltpu.VMEM((DEV, 3, 1, COLS), f32),
            pltpu.VMEM((DEV, 3, 1, COLS), f32),
            pltpu.VMEM((2, 32, 2, 1, COLS), f32),
            pltpu.VMEM((2, 32, 2, 1, COLS), f32),
            dma((LOADS,)), dma((3,)), dma((2,)), dma((2,)), dma((2,)), dma((2,)),
            dma, dma, dma, dma,
        ],
        name="sketch",
        compiler_params=pltpu.CompilerParams(
            collective_id=1, has_side_effects=True, vmem_limit_bytes=56 * 2**20
        ),
    )(panel, flips.reshape(32, 128), picks.reshape(64, 128))
    return pl.pallas_call(
        leave_kernel,
        out_shape=tuple(jax.ShapeDtypeStruct(shape, f32) for shape in shapes),
        in_specs=[vmem, vmem, vmem],
        out_specs=(hbm, hbm, hbm),
        scratch_shapes=[dma((3,))],
        name="leave",
    )(*(pltpu.with_memory_space_constraint(p, pltpu.VMEM) for p in parts))


def solution(mesh):
    both = ("narrow", "wide")
    return jax.shard_map(
        on_device,
        mesh=mesh,
        in_specs=(P(both, None), P(both), P()),
        out_specs=(P(both, None), P(both, None), P()),
        check_vma=False,
    )
```

```python
import itertools

import jax
import jax.numpy as jnp
from jax import lax
from jax.experimental import pallas as pl
from jax.experimental.pallas import tpu as pltpu
from jax.sharding import PartitionSpec as P

MESH = pl.DeviceIdType.MESH
DEV = 128
ROWS = 4096
COLS = 128
CHUNK = 32
HALF = 16
LOADS = 4
SCALE = 1.0 / float(ROWS * DEV) ** 0.5


def offsets():
    rest = [o for o in itertools.product(range(4), range(4), range(4), range(2)) if any(o)]
    used = [0] * 6
    order = []

    def load(o):
        out = [0] * 6
        for i in range(3):
            out[2 * i] = (0, 1, 1, 0)[o[i]]
            out[2 * i + 1] = (0, 0, 1, 1)[o[i]]
        return out

    def cost(o):
        total = [u + w for u, w in zip(used, load(o))]
        return -sum(load(o)), max(total) - min(total), max(total)

    while rest:
        best = min(rest, key=cost)
        rest.remove(best)
        order.append(best)
        used = [u + w for u, w in zip(used, load(best))]
    return order


OFFSETS = offsets()
FAR_FIRST = OFFSETS
CROSS = [o for o in OFFSETS if o[3] == 1 and sum(min(v, 4 - v) for v in o[:3]) == 1]
OFFSETS = CROSS + [o for o in OFFSETS if o not in CROSS]


class Place:
    def __init__(self):
        self.narrow, self.wide = lax.axis_index("narrow"), lax.axis_index("wide")
        self.me = self.narrow * 32 + self.wide
        y, z_lo, x = self.wide & 3, (self.wide >> 2) & 1, self.wide >> 3
        core, z = self.narrow & 1, (self.narrow >> 1) * 2 + z_lo
        self.xs = [((x + i) & 3) * 8 for i in range(4)]
        self.ys = [(y + i) & 3 for i in range(4)]
        self.zs = [((z + i) & 1) * 4 for i in range(4)]
        self.zn = [(((z + i) >> 1) & 1) * 2 for i in range(4)]
        self.cs = [core, 1 - core]

    def others(self, offsets=OFFSETS):
        for dx, dy, dz, dc in offsets:
            narrow, wide = self.zn[dz] + self.cs[dc], self.xs[dx] + self.ys[dy] + self.zs[dz]
            yield narrow * 32 + wide, (narrow, wide)


def butterfly(values):
    values = list(values)
    apart = 1
    while apart < len(values):
        for i in range(len(values)):
            if i & apart == 0:
                a, b = values[i], values[i + apart]
                values[i], values[i + apart] = a + b, a - b
        apart *= 2
    return values


def first_pass(x_ref, signs, t_ref, g):
    rows = x_ref[g * 128 : g * 128 + 128, :] * signs[:, g : g + 1]
    out = butterfly([rows[8 * m : 8 * m + 8] for m in range(16)])
    for m in range(16):
        t_ref[g * 128 + 8 * m : g * 128 + 8 * m + 8, :] = out[m]


def second_pass(t_ref):
    def step(g, carry):
        base = (g // 2) * 256 + (g % 2) * 64
        spots = [base + 128 * h + k for h in range(2) for k in range(8)]
        out = butterfly([t_ref[pl.ds(s, 8, stride=8), :] for s in spots])
        for s, value in zip(spots, out):
            t_ref[pl.ds(s, 8, stride=8), :] = value
        return carry

    lax.fori_loop(0, 32, step, 0, unroll=8)


def third_pass(half, t_ref):
    def step(g, carry):
        base = pl.multiple_of((g % 2) * 8 + half * HALF + (g // 2) * CHUNK, 8)
        spots = [base + 256 * m for m in range(16)]
        out = butterfly([t_ref[pl.ds(s, 8), :] for s in spots])
        for s, value in zip(spots, out):
            t_ref[pl.ds(s, 8), :] = value
        return carry

    lax.fori_loop(0, 16, step, 0, unroll=8)


def device_transform(half, src_ref, dst_ref):
    def low(g, carry):
        for u in range(2):
            rows = pl.ds(half * HALF + 8 * u, 8)
            out = butterfly([src_ref[g * 16 + m, rows, :] for m in range(16)])
            for m in range(16):
                dst_ref[g * 16 + m, rows, :] = out[m]
        return carry

    lax.fori_loop(0, 8, low, 0, unroll=2)

    def high(g, carry):
        for u in range(2):
            rows = pl.ds(half * HALF + 8 * u, 8)
            out = butterfly([dst_ref[g + 16 * m, rows, :] for m in range(8)])
            for m in range(8):
                dst_ref[g + 16 * m, rows, :] = out[m] * SCALE
        return carry

    lax.fori_loop(0, 16, high, 0, unroll=4)


def counts_of(me, picks_ref):
    def step(k, total):
        p = picks_ref[pl.ds(k, 1), :]
        here = ((p >> 5) & 127) == me
        q = ((p >> 4) & 1) * (DEV * HALF) + (p >> 12) * HALF + (p & 15)
        hi = jnp.where(here, q >> 7, -1)
        lo = q & 127
        a = (lax.broadcasted_iota(jnp.int32, (32, 128), 0) == hi).astype(jnp.float32)
        b = (lax.broadcasted_iota(jnp.int32, (128, 128), 0) == lo).astype(jnp.float32)
        return total + lax.dot_general(
            a, b, (((1,), (1,)), ((), ())), preferred_element_type=jnp.float32
        )

    return lax.fori_loop(0, 64, step, jnp.zeros((32, 128), jnp.float32))


def kernel(
    panel_ref, flips_hbm, picks_hbm,
    mixed_ref, sketch_ref, gram_ref,
    x_ref, t_ref, in_ref, done_ref, flips_ref, picks_ref, counts_ref, part_ref, wanted_ref, wanted_sm, mine_sm,
    row_out, row_in, gp_out, gp_in,
    load_sem, small_sem, p1s, p1r, p2s, p2r, gps, gpr, rows_s, rows_r,
):
    here = Place()
    me = here.me
    barrier = pltpu.get_barrier_semaphore()
    for _, spot in here.others(FAR_FIRST):
        pl.semaphore_signal(barrier, inc=1, device_id=spot, device_id_type=MESH)
    small = [
        pltpu.make_async_copy(flips_hbm, flips_ref, small_sem.at[0]),
        pltpu.make_async_copy(picks_hbm, picks_ref, small_sem.at[1]),
        pltpu.make_async_copy(picks_hbm.at[me >> 1], mine_sm, small_sem.at[2]),
    ]
    small[0].start()
    loads = []
    for i in range(LOADS):
        rows = pl.ds(i * (ROWS // LOADS), ROWS // LOADS)
        loads.append(pltpu.make_async_copy(panel_ref.at[rows], x_ref.at[rows], load_sem.at[i]))
        loads[-1].start()
    small[1].start()
    small[2].start()
    small[0].wait()
    signs = (1 - 2 * flips_ref[...]).astype(jnp.float32).T
    for g in range(32):
        if g % (32 // LOADS) == 0:
            loads[g // (32 // LOADS)].wait()
        first_pass(x_ref, signs, t_ref, g)
    second_pass(t_ref)
    third_pass(0, t_ref)
    pl.semaphore_wait(barrier, DEV - 1)

    def rows_of(d, half):
        return pl.ds(pl.multiple_of(d * CHUNK + half * HALF, HALF), HALF)

    def send(src, dst, send_sem, recv_sem, spot):
        pltpu.make_async_remote_copy(
            src, dst, send_sem, recv_sem, device_id=spot, device_id_type=MESH
        ).start()

    def send_in(half):
        part = pl.ds(half * HALF, HALF)
        for d, spot in here.others():
            send(t_ref.at[rows_of(d, half)], in_ref.at[me, part], p1s.at[half], p1r.at[half], spot)

    def send_back(half):
        part = pl.ds(half * HALF, HALF)
        for d, spot in here.others():
            send(done_ref.at[d, part], mixed_ref.at[rows_of(me, half)], p2s.at[half], p2r.at[half], spot)

    def wait_bytes(sem):
        others = pl.ds(0, (DEV - 1) * HALF)
        pltpu.make_async_copy(x_ref.at[others], t_ref.at[others], sem).wait()

    def wait_rows(ref, sem):
        pltpu.make_async_copy(ref.at[pl.ds(0, DEV - 1)], ref.at[pl.ds(0, DEV - 1)], sem).wait()

    def add_gram(half):
        def step(g, total):
            rows = done_ref[pl.ds(g * 8, 8), pl.ds(half * HALF, HALF), :].reshape(128, COLS)
            left = rows.T * counts_ref[pl.ds(half * 16 + g, 1), :]
            return total + jnp.dot(
                left, rows, precision=lax.Precision.HIGHEST, preferred_element_type=jnp.float32
            )

        part_ref[...] = lax.fori_loop(0, 16, step, part_ref[...], unroll=4)

    send_in(0)
    third_pass(1, t_ref)
    send_in(1)
    in_ref[me] = t_ref[pl.ds(pl.multiple_of(me * CHUNK, CHUNK), CHUNK), :]

    small[1].wait()
    p = picks_ref[...]
    lane = lax.broadcasted_iota(jnp.int32, p.shape, 1)
    local = jnp.where((p >> 12) == me, p & (ROWS - 1), 0)
    even = jnp.max(jnp.where(lane < 64, local, 0), axis=1, keepdims=True)
    odd = jnp.max(jnp.where(lane < 64, 0, local), axis=1, keepdims=True)
    wanted_ref[...] = jnp.where(lane == 0, even, odd)
    wanted = pltpu.make_async_copy(wanted_ref, wanted_sm, small_sem.at[1])
    wanted.start()
    counts_ref[...] = counts_of(me, picks_ref)
    part_ref[...] = jnp.zeros_like(part_ref)

    wait_bytes(p1r.at[0])
    device_transform(0, in_ref, done_ref)
    send_back(0)
    add_gram(0)
    wait_bytes(p1r.at[1])
    device_transform(1, in_ref, done_ref)
    add_gram(1)
    gp_out[...] = part_ref[...].reshape(DEV, 1, COLS)
    for d, spot in here.others():
        send(gp_out.at[d], gp_in.at[me], gps, gpr, spot)
    send_back(1)
    gp_in[me] = gp_out[me]
    mixed_ref[pl.ds(pl.multiple_of(me * CHUNK, CHUNK), CHUNK), :] = done_ref[me]
    wait_rows(gp_in, gpr)
    gram_row = jnp.sum(gp_in[...], axis=0, keepdims=True) * (1.0 / 8192.0)
    row_out[:, 1] = jnp.broadcast_to(gram_row, (DEV, 1, COLS))

    wanted.wait()
    wait_bytes(p2r.at[0])
    wait_bytes(p2r.at[1])

    def gather(k, carry):
        for j in range(2):
            row_out[2 * k + j, 0] = mixed_ref[pl.ds(wanted_sm[k, j], 1), :]
        return carry

    lax.fori_loop(0, DEV // 2, gather, 0, unroll=8)
    for d, spot in here.others():
        send(row_out.at[d], row_in.at[me], rows_s, rows_r, spot)
    row_in[me] = row_out[me]
    small[2].wait()
    for half in range(2):
        wait_bytes(p1s.at[half])
        wait_bytes(p2s.at[half])
    wait_rows(gp_in, gps)
    wait_rows(row_in, rows_r)
    start = (me & 1) * 64

    def pick_row(i, carry):
        sketch_ref[pl.ds(i, 1), :] = row_in[(mine_sm[start + i] >> 12) & (DEV - 1), 0]
        return carry

    lax.fori_loop(0, 64, pick_row, 0, unroll=16)
    gram_ref[...] = row_in[:, 1].reshape(COLS, COLS)
    wait_rows(row_in, rows_s)


def leave_kernel(mixed_ref, sketch_ref, gram_ref, mixed_out, sketch_out, gram_out, sems):
    n = ROWS // 2
    pairs = tuple((mixed_ref.at[pl.ds(i * n, n)], mixed_out.at[pl.ds(i * n, n)]) for i in range(2)) + ((sketch_ref, sketch_out), (gram_ref, gram_out))
    copies = [pltpu.make_async_copy(a, b, sems.at[i]) for i, (a, b) in enumerate(pairs)]
    for i, copy in enumerate(copies):
        copy.start(priority=i % 2)
    for copy in copies:
        copy.wait()


def on_device(panel, flips, picks):
    vmem = pl.BlockSpec(memory_space=pltpu.VMEM)
    hbm = pl.BlockSpec(memory_space=pltpu.HBM)
    dma = pltpu.SemaphoreType.DMA
    f32, i32 = jnp.float32, jnp.int32
    shapes = ((ROWS, COLS), (64, COLS), (COLS, COLS))
    parts = pl.pallas_call(
        kernel,
        out_shape=tuple(pltpu.VMEM(shape, f32) for shape in shapes),
        in_specs=[hbm, hbm, hbm],
        out_specs=(vmem, vmem, vmem),
        scratch_shapes=[
            pltpu.VMEM((ROWS, COLS), f32),
            pltpu.VMEM((ROWS, COLS), f32),
            pltpu.VMEM((DEV, CHUNK, COLS), f32),
            pltpu.VMEM((DEV, CHUNK, COLS), f32),
            pltpu.VMEM((32, 128), i32),
            pltpu.VMEM((64, 128), i32),
            pltpu.VMEM((32, 128), f32),
            pltpu.VMEM((COLS, COLS), f32),
            pltpu.VMEM((64, 128), i32),
            pltpu.SMEM((64, 128), i32),
            pltpu.SMEM((128,), i32),
            pltpu.VMEM((DEV, 2, 1, COLS), f32),
            pltpu.VMEM((DEV, 2, 1, COLS), f32),
            pltpu.VMEM((DEV, 1, COLS), f32),
            pltpu.VMEM((DEV, 1, COLS), f32),
            dma((LOADS,)), dma((3,)), dma((2,)), dma((2,)), dma((2,)), dma((2,)),
            dma, dma, dma, dma,
        ],
        name="sketch",
        compiler_params=pltpu.CompilerParams(
            collective_id=1, has_side_effects=True, vmem_limit_bytes=56 * 2**20
        ),
    )(panel, flips.reshape(32, 128), picks.reshape(64, 128))
    return pl.pallas_call(
        leave_kernel,
        out_shape=tuple(jax.ShapeDtypeStruct(shape, f32) for shape in shapes),
        in_specs=[vmem, vmem, vmem],
        out_specs=(hbm, hbm, hbm),
        scratch_shapes=[dma((4,))],
        name="leave",
    )(*(pltpu.with_memory_space_constraint(p, pltpu.VMEM) for p in parts))


def solution(mesh):
    both = ("narrow", "wide")
    return jax.shard_map(
        on_device,
        mesh=mesh,
        in_specs=(P(both, None), P(both), P()),
        out_specs=(P(both, None), P(both, None), P()),
        check_vma=False,
    )
```
